32 devices in a mesh: dp: 4 (over y, core), expert: 8 (over z, x).
Axes of the slice: x: 2, y: 2, z: 4, core: 2. Of those that a mesh axis runs over, the one named last changes fastest.
Arguments:
- tokens: bfloat16 [4, 1024, 2, 2048], P('dp', 'expert'), may hold values from -6 to 6
- lengths: int32 [4, 2], replicated, may hold values from 256 to 1024, as said below
- routes: int32 [4, 1024, 2, 8], P('dp', 'expert'), may hold values from 0 to 15, all different within a row; in each aligned block of 256 rows (0 to 255, 256 to 511, ..., all dimensions but the last counted through in order) at most 192 rows name the same one
- attn_gain: float32 [2048], replicated, may hold values from 0.25 to 1.75
- q_gain: float32 [128], replicated, may hold values from 0.25 to 1.75
- k_gain: float32 [128], replicated, may hold values from 0.25 to 1.75
- qkv_weight: bfloat16 [2048, 3, 2048], P(('dp', 'expert')), may hold values from -0.125 to 0.125
- out_weight: bfloat16 [2048, 2048], P(('dp', 'expert')), may hold values from -2.5 to 2.5
- ffn_gain: float32 [2048], replicated, may hold values from 0.25 to 1.75
- router_weight: bfloat16 [2048, 16], replicated, may hold values from -0.0625 to 0.0625
- expert_in: bfloat16 [16, 2048, 2048], P('expert'), may hold values from -0.125 to 0.125
- expert_out: bfloat16 [16, 1024, 2048], P('expert'), may hold values from -0.75 to 0.75
- balance_coef: float32 [1], replicated, may hold values from 0.5 to 1.5
- cotangent: bfloat16 [4, 1024, 2, 2048], P('dp', 'expert'), may hold values from -6 to 6
Outputs:
- block_out: float32 [4, 1024, 2, 2048], P('dp', 'expert')
- balance_loss: float32 [1], replicated
- grad_tokens: float32 [4, 1024, 2, 2048], P('dp', 'expert')
- grad_attn_gain: float32 [2048], replicated
- grad_q_gain: float32 [128], replicated
- grad_k_gain: float32 [128], replicated
- grad_qkv: float32 [2048, 3, 2048], P(('dp', 'expert'))
- grad_out_weight: float32 [2048, 2048], P(('dp', 'expert'))
- grad_ffn_gain: float32 [2048], replicated
- grad_router: float32 [2048, 16], replicated
- grad_expert_in: float32 [16, 2048, 2048], P('expert', 'dp')
- grad_expert_out: float32 [16, 1024, 2048], P('expert', 'dp')
The draws below stay inside these ranges and needn't reach their ends.
Inputs may be any that keep to these rules, and one draw needn't show every extreme that they name: `routes`: each row names 8 different experts. In the rows of one device, aligned blocks of 256 rows in the order group, slot, sequence, no expert is named by more than 192 rows. `lengths`: in each group one of the 2 sequences, which one varies, holds all 1024 slots.
All inputs are finite; a program needn't handle non-finite values.
Results may differ from the reference program's by a relative error of at most 0.02.
Values may be sent and summed in bfloat16 or wider, within the bound.
No kernel may reach another device: no remote copies, remote signals or barrier semaphores. Data moves between devices by JAX's collectives and lax.ppermute only.
A program may use at most 384 MiB of HBM per device.

```python
import math
import jax
import jax.numpy as jnp
import numpy as np
from jax import lax

D = 2048
HEADS = 16
HD = 128
FF = 1024
TOPK = 8
SEQ = 1024
SEQS_GRP = 2
EXPERTS = 16
TOK_DEV = 256
CAP = 192
N_DP = 4


def draw_lengths(key, part):
    key = jax.random.fold_in(key, 7)
    full_key, rest_key = jax.random.split(key)
    full_index = jax.random.randint(full_key, (N_DP,), 0, SEQS_GRP)
    other_len = jax.random.randint(rest_key, (N_DP, SEQS_GRP), SEQ // 4, SEQ + 1)
    columns = jnp.arange(SEQS_GRP)
    return jnp.where(columns[None, :] == full_index[:, None], SEQ, other_len).astype(jnp.int32)


def block_scale(own_key, shape, cuts, low, high):
    factor_of, own = 1.0, jax.random.fold_in(own_key, 6)
    for dim, parts in cuts:
        steps = jnp.exp(jax.random.uniform(jax.random.fold_in(own, dim), (parts,), jnp.float32, low / len(cuts), high / len(cuts)))
        factor_of = factor_of * jnp.repeat(steps, shape[dim] // parts).reshape([-1 if axis == dim else 1 for axis in range(len(shape))])
    return factor_of


def shared_out(rng, own, number, rows, count, top, bound, skew):
    order = jax.random.permutation(rng, count)
    heavy_load, ordinary = portions_of(count, rows * top, bound, skew, True), portions_of(count, rows * top, bound, skew, False)
    places = jnp.arange(count)

    def named(tallies, rotation):
        used = int((tallies > 0).sum())
        fixed = max(1, used // 4)
        shifted = fixed + (places - fixed + rotation * (used - fixed)) % max(1, count - fixed)
        return jnp.zeros((count,), jnp.int32).at[order[jnp.where(places < fixed, places, shifted)]].set(jnp.asarray(tallies, jnp.int32))

    tallies = jnp.where(number % 4 == 0, named(heavy_load, number // 4), named(ordinary, number - number // 4 - 1))
    mixed = jax.random.permutation(jax.random.fold_in(own, 3), count)
    donor, receiver = mixed[0:count // 2 * 2:2], mixed[1:count // 2 * 2:2]
    slack = jnp.minimum(tallies[donor] - 1, bound - tallies[receiver]) // 2
    slack = jnp.where((donor == order[0]) | (receiver == order[0]) | (tallies[receiver] == 0), 0, jnp.maximum(slack, 0))
    shifted = jax.random.randint(jax.random.fold_in(own, 4), (count // 2,), 0, 1 << 20) % (slack + 1)
    tallies = tallies.at[donor].add(-shifted).at[receiver].add(shifted)
    items = jnp.searchsorted(jnp.cumsum(tallies), jnp.arange(rows * top), side="right").astype(jnp.int32)
    grid = items.reshape(top, rows).T
    grid = grid[jax.random.permutation(jax.random.fold_in(own, 1), rows)]
    rotation = jax.random.randint(jax.random.fold_in(own, 2), (rows, 1), 0, top)
    return jnp.take_along_axis(grid, (jnp.arange(top)[None, :] + rotation) % top, axis=1)


def portions_of(amount, total, most, slope, full):
    portions = [(1 << 20) // math.isqrt(rank ** slope) + 1 for rank in range(1, amount + 1)]
    largest = most if full else min(most, max(-(-total // amount), total * portions[0] // sum(portions)))
    least = 1 if total - largest >= amount - 1 else 0
    counts, surplus = [largest] + [least] * (amount - 1), total - largest - least * (amount - 1)
    while surplus > 0:
        candidates = [i for i in range(1, amount) if counts[i] < largest] or [i for i in range(1, amount) if counts[i] < most]
        whole, left = sum([portions[i] for i in candidates]), surplus
        for i in candidates:
            addition = min(most - counts[i], max(1, left * portions[i] // whole), surplus)
            counts[i] = counts[i] + addition
            surplus = surplus - addition
    return np.array(counts)


def centred(key, dims, deviation, reach, shards=(), kind=jnp.bfloat16):
    entries = jax.random.normal(key, dims, jnp.float32) * deviation
    if len(shards) > 0:
        entries = block_scale(key, dims, shards, -0.22, 0.18) * entries
    return jnp.clip(entries, min=-reach, max=reach).astype(kind)


def setup_inputs(seed: int = 0) -> dict:
    splits = jax.random.split(jax.random.key(seed), 15)
    tokens = centred(splits[0], (N_DP, SEQ, SEQS_GRP, D), 1.0, 6.0, ((0, 4), (1, 8)))
    lengths = draw_lengths(jax.random.fold_in(splits[14], 71), 0)
    routes_keys = jax.random.split(jax.random.fold_in(splits[2], 1), N_DP * SEQ * SEQS_GRP // TOK_DEV)
    routes_turns = jax.random.permutation(jax.random.fold_in(splits[2], 3), N_DP * SEQ * SEQS_GRP // TOK_DEV)
    routes = jax.vmap(lambda own, number: shared_out(jax.random.fold_in(splits[2], 2), own, number, TOK_DEV, EXPERTS, TOPK, CAP, 1))(routes_keys, routes_turns).reshape((N_DP, SEQ, SEQS_GRP, TOPK))
    attn_gain = jnp.clip(1.0 + 0.15 * jax.random.normal(splits[3], (D,), jnp.float32), 0.25, 1.75)
    q_gain = jnp.clip(1.0 + 0.15 * jax.random.normal(splits[4], (HD,), jnp.float32), 0.25, 1.75)
    k_gain = jnp.clip(1.0 + 0.15 * jax.random.normal(splits[5], (HD,), jnp.float32), 0.25, 1.75)
    qkv_weight = centred(splits[6], (D, 3, D), D ** -0.5, 0.125, ((0, 32),))
    out_weight = centred(splits[7], (D, D), (max(3 * D // SEQ, 1)) ** -0.5, 2.5, ((0, 32),))
    ffn_gain = jnp.clip(1.0 + 0.15 * jax.random.normal(splits[8], (D,), jnp.float32), 0.25, 1.75)
    router_weight = centred(splits[9], (D, EXPERTS), (0.5 / D ** 0.5), 0.0625)
    expert_in = centred(splits[10], (EXPERTS, D, 2 * FF), D ** -0.5, 0.125, ((0, 8),))
    expert_out = centred(splits[11], (EXPERTS, FF, D), (FF // 16) ** -0.5, 0.75, ((0, 8),))
    balance_coef = jnp.clip(jax.random.uniform(splits[12], (1,), jnp.float32, 0.5, 1.5), 0.5, 1.5)
    cotangent = centred(splits[13], (N_DP, SEQ, SEQS_GRP, D), 1.0, 6.0, ((0, 4), (1, 8)))
    return {"tokens": tokens, "lengths": lengths, "routes": routes, "attn_gain": attn_gain, "q_gain": q_gain, "k_gain": k_gain, "qkv_weight": qkv_weight, "out_weight": out_weight, "ffn_gain": ffn_gain, "router_weight": router_weight, "expert_in": expert_in, "expert_out": expert_out, "balance_coef": balance_coef, "cotangent": cotangent}


@jax.custom_vjp
def low(v):
    return lax.optimization_barrier(v.astype(jnp.bfloat16)).astype(jnp.float32)

@jax.custom_vjp
def low_back(v):
    return v

def low_keep(v):
    return (low(v), None)

def low_pass(kept, grad):
    return (grad,)

def back_keep(v):
    return (v, None)

def back_low(kept, grad):
    return (low(grad),)
low.defvjp(low_keep, low_pass)
low_back.defvjp(back_keep, back_low)
NORM_EPS = 1e-05
PRECISE = lax.Precision.HIGHEST

def norm_rows(values, scale_gain):
    return values * lax.rsqrt(lax.optimization_barrier(jnp.mean(values * values, axis=-1, keepdims=True)) + NORM_EPS) * scale_gain

def rotary(values, positions):
    half_width = values.shape[-1] // 2
    inv_freq = jnp.exp(jnp.arange(half_width, dtype=jnp.float32) * (-2.0 * math.log(10000.0) / values.shape[-1]))
    angles = positions[:, None] * inv_freq[None, :]
    cosine = jnp.cos(angles)[:, None, None, :]
    sine = jnp.sin(angles)[:, None, None, :]
    first_half = values[..., :half_width]
    second_half = values[..., half_width:]
    return jnp.concatenate([first_half * cosine - second_half * sine, second_half * cosine + first_half * sine], axis=-1)

def attend_group(x_group, len_group, attn_gain, q_gain, k_gain, w_qkv, w_out):
    seq_len = x_group.shape[0]
    seq_count = x_group.shape[1]
    positions = jnp.arange(seq_len, dtype=jnp.float32)
    head_shape = (seq_len, seq_count, HEADS, HD)
    normed = low(norm_rows(x_group, attn_gain))
    project = low_back(jnp.einsum('tsd,dcf->tscf', normed, w_qkv, precision=PRECISE))
    queries = low(rotary(norm_rows(project[:, :, 0].reshape(head_shape), q_gain), positions))
    key_rows = low(rotary(norm_rows(project[:, :, 1].reshape(head_shape), k_gain), positions))
    values = low(project[:, :, 2].reshape(head_shape))
    scores = low_back(jnp.einsum('tshd,ushd->shtu', queries, key_rows, precision=PRECISE) / math.sqrt(HD))
    key_live = jnp.arange(seq_len)[None, :] < len_group[:, None]
    scores = jnp.where(key_live[:, None, None, :], scores, -1e+30)
    highest = lax.optimization_barrier(jnp.max(scores, axis=-1, keepdims=True))
    expo_scores = jnp.exp(scores - highest)
    attn_probs = expo_scores / lax.optimization_barrier(jnp.sum(expo_scores, axis=-1, keepdims=True))
    attended = jnp.einsum('shtu,ushd->tshd', low(attn_probs), values, precision=PRECISE).reshape(seq_len, seq_count, D)
    attended = low_back(low(attended))
    branch = low_back(jnp.einsum('tsd,de->tse', attended, w_out, precision=PRECISE))
    return x_group + branch

def expert_block(rows_block, picks_block, gates_block, w_in, w_down):
    expert_hits = (picks_block[:, None] == jnp.arange(EXPERTS)[None, :]).astype(jnp.int32)
    slot_order = lax.optimization_barrier(jnp.sum((jnp.cumsum(expert_hits, axis=0) - 1) * expert_hits, axis=1)).astype(jnp.int32)
    slot_index = (picks_block * CAP + slot_order).astype(jnp.int32)
    source_row = (jnp.arange(picks_block.shape[0]) // TOPK).astype(jnp.int32)
    buffer = jnp.zeros((EXPERTS * CAP, D), rows_block.dtype).at[slot_index].set(rows_block[source_row])
    buffer = low_back(buffer.reshape(EXPERTS, CAP, D))
    gate_up = low_back(jnp.einsum('ecd,edf->ecf', buffer, w_in, precision=PRECISE))
    hidden = low(jax.nn.silu(gate_up[..., :FF]) * gate_up[..., FF:])
    result = low_back(low(jnp.einsum('ecf,efd->ecd', hidden, w_down, precision=PRECISE)))
    paired = result.reshape(EXPERTS * CAP, D)[slot_index].reshape(TOK_DEV, TOPK, D)
    return lax.optimization_barrier(jnp.sum(gates_block[:, :, None] * paired, axis=1))

def reference(tokens, lengths, routes, attn_gain, q_gain, k_gain, qkv_weight, out_weight, ffn_gain, router_weight, expert_in, expert_out, balance_coef, cotangent):
    valid_mask = (jnp.arange(SEQ)[None, :, None] < lengths[:, None, :]).astype(jnp.float32)
    valid_rows = valid_mask.reshape(-1)
    n_valid = jnp.sum(lengths).astype(jnp.float32)
    picked_ids = routes.reshape(-1, TOPK)
    chosen = (picked_ids[:, :, None] == jnp.arange(EXPERTS)[None, None, :]).astype(jnp.float32)
    fraction = lax.optimization_barrier(jnp.sum(valid_rows[:, None, None] * chosen, axis=(0, 1))) / (TOPK * n_valid)

    def forward(inputs, g_attn, g_query, g_key, w_qkv, w_out, g_ffn, w_router, w_in, w_down):

        def group_step(carried, group_data):
            x_group, len_group = group_data
            return (carried, attend_group(x_group, len_group, g_attn, g_query, g_key, w_qkv, w_out))
        _, residual = lax.scan(jax.checkpoint(group_step), jnp.zeros((), jnp.float32), (inputs, lengths))
        flat_rows = residual.reshape(-1, D)
        ffn_normed = low(norm_rows(flat_rows, g_ffn))
        logits = jnp.dot(ffn_normed, w_router, precision=PRECISE)
        router_probs = jax.nn.softmax(logits, axis=-1)
        picked = jnp.take_along_axis(router_probs, picked_ids, axis=1)
        gate_weights = valid_rows[:, None] * picked / lax.optimization_barrier(jnp.sum(picked, axis=-1, keepdims=True))
        mean_prob = lax.optimization_barrier(jnp.sum(valid_rows[:, None] * router_probs, axis=0)) / n_valid
        balance_loss = balance_coef * EXPERTS * jnp.sum(fraction * mean_prob)

        def expert_step(carried, block_data):
            rows_block, picks_block, gates_block = block_data
            return (carried, expert_block(rows_block, picks_block, gates_block, w_in, w_down))
        block_data = (ffn_normed.reshape(-1, TOK_DEV, D), picked_ids.reshape(-1, TOK_DEV * TOPK), gate_weights.reshape(-1, TOK_DEV, TOPK))
        _, mixture = lax.scan(jax.checkpoint(expert_step), jnp.zeros((), jnp.float32), block_data)
        block_out = (flat_rows + mixture.reshape(-1, D)).reshape(inputs.shape)
        return (block_out, balance_loss)
    primals = (tokens.astype(jnp.float32), attn_gain.astype(jnp.float32), q_gain.astype(jnp.float32), k_gain.astype(jnp.float32), qkv_weight.astype(jnp.float32), out_weight.astype(jnp.float32), ffn_gain.astype(jnp.float32), router_weight.astype(jnp.float32), expert_in.astype(jnp.float32), expert_out.astype(jnp.float32))
    (block_out, balance_loss), pullback = jax.vjp(forward, *primals)
    gradients = pullback((cotangent.astype(jnp.float32) * valid_mask[..., None], jnp.ones((1,), jnp.float32)))
    return (block_out, balance_loss, gradients[0], gradients[1], gradients[2], gradients[3], gradients[4], gradients[5], gradients[6], gradients[7], gradients[8], gradients[9])
```

```python
import math

import jax
import jax.numpy as jnp
from jax import lax
from jax.sharding import PartitionSpec as P

HEADS = 16
HD = 128
FF = 1024
TOPK = 8


NORM_EPS = 1e-05
PRECISE = lax.Precision.HIGHEST


def norm_rows(values, scale_gain):
    return (
        values
        * lax.rsqrt(jnp.mean(values * values, axis=-1, keepdims=True) + NORM_EPS)
        * scale_gain
    )


def rotary(values, positions):
    half_width = values.shape[-1] // 2
    inv_freq = jnp.exp(
        jnp.arange(half_width, dtype=jnp.float32) * (-2.0 * math.log(10000.0) / values.shape[-1])
    )
    angles = positions[:, None] * inv_freq[None, :]
    cosine = jnp.cos(angles)[:, None, None, :]
    sine = jnp.sin(angles)[:, None, None, :]
    first_half = values[..., :half_width]
    second_half = values[..., half_width:]
    return jnp.concatenate(
        [first_half * cosine - second_half * sine, second_half * cosine + first_half * sine],
        axis=-1,
    )


def body(
    tokens,
    lengths,
    routes,
    attn_gain,
    q_gain,
    k_gain,
    qkv_weight,
    out_weight,
    ffn_gain,
    router_weight,
    expert_in,
    expert_out,
    balance_coef,
    cotangent,
):
    bf16, f32 = jnp.bfloat16, jnp.float32
    n_expert = lax.axis_size("expert")
    group_index = lax.axis_index("dp")
    member = lax.axis_index("expert")
    slot_count = tokens.shape[1]
    seq_count = tokens.shape[2]
    width = tokens.shape[3]
    experts_here = expert_in.shape[0]
    experts_all = experts_here * n_expert
    tok_rows = slot_count * seq_count
    full_len = slot_count * n_expert
    all_rows = tok_rows * n_expert
    heads_here = HEADS // n_expert
    cols = heads_here * HD
    head_shape = (full_len, seq_count, heads_here, HD)
    scale = 1.0 / math.sqrt(HD)

    def gather_rows(rows):
        return lax.all_gather(rows, "expert", axis=0, tiled=True)

    def scatter_rows(rows):
        return lax.psum_scatter(rows, "expert", scatter_dimension=0, tiled=True)

    slot_ids = member * slot_count + jnp.arange(slot_count)
    seq_lens = lengths[group_index]
    valid_mask = (slot_ids[:, None] < seq_lens[None, :]).astype(f32)
    valid_rows = valid_mask.reshape(tok_rows)
    all_slots = jnp.arange(full_len)
    positions = all_slots.astype(f32)
    key_live = all_slots[None, :] < seq_lens[:, None]
    valid_all = (all_slots[:, None] < seq_lens[None, :]).astype(f32).reshape(all_rows)

    picked_ids = routes.reshape(tok_rows, TOPK)
    chosen = jnp.sum(
        (picked_ids[:, :, None] == jnp.arange(experts_all)[None, None, :]).astype(f32), axis=1
    )
    counts = jnp.sum(valid_rows[:, None] * chosen, axis=0)
    count_total = lax.psum(counts, ("dp", "expert"))
    n_valid = jnp.sum(lengths).astype(f32)
    fraction = count_total / (TOPK * n_valid)
    chosen_all = gather_rows(chosen)

    row_count = qkv_weight.shape[0]
    w_cols = lax.all_to_all(
        qkv_weight.reshape(row_count, 3, n_expert, cols),
        "expert",
        split_axis=2,
        concat_axis=0,
        tiled=True,
    ).reshape(n_expert * row_count, 3 * cols)
    w_qkv = lax.all_gather(w_cols, "dp", axis=0, tiled=True)
    w_out = lax.all_gather(
        lax.all_gather(out_weight, "expert", axis=0, tiled=True), "dp", axis=0, tiled=True
    )

    inputs = tokens[0].astype(f32).reshape(tok_rows, width)
    normed, norm_back = jax.vjp(norm_rows, inputs, attn_gain)
    normed_all = gather_rows(normed.astype(bf16))
    project = jnp.dot(normed_all, w_qkv, preferred_element_type=f32)

    def shape_heads(query_proj, key_proj, query_gain, key_gain):
        return (
            rotary(norm_rows(query_proj.reshape(head_shape), query_gain), positions),
            rotary(norm_rows(key_proj.reshape(head_shape), key_gain), positions),
        )

    (query_full, key_full), heads_back = jax.vjp(
        shape_heads, project[:, :cols], project[:, cols : 2 * cols], q_gain, k_gain
    )
    queries = query_full.astype(bf16)
    key_rows = key_full.astype(bf16)
    values = project[:, 2 * cols :].reshape(head_shape).astype(bf16)

    def scores_of():
        raw_scores = (
            jnp.einsum("tshd,ushd->shtu", queries, key_rows, preferred_element_type=f32) * scale
        )
        return jnp.where(key_live[:, None, None, :], raw_scores, -1e30)

    scores = scores_of()
    highest = jnp.max(scores, axis=-1, keepdims=True)
    expo_scores = jnp.exp(scores - highest)
    totals = jnp.sum(expo_scores, axis=-1, keepdims=True)
    log_total = highest + jnp.log(totals)
    probs_low = (expo_scores / totals).astype(bf16)
    attended = jnp.einsum("shtu,ushd->tshd", probs_low, values, preferred_element_type=f32)
    attended_heads = attended.astype(bf16).reshape(n_expert, tok_rows, cols)
    attended_low = (
        lax.all_to_all(attended_heads, "expert", split_axis=0, concat_axis=0, tiled=True)
        .transpose(1, 0, 2)
        .reshape(tok_rows, width)
    )
    residual = inputs + jnp.dot(attended_low, w_out, preferred_element_type=f32)
    ffn_normed, ffn_back = jax.vjp(norm_rows, residual, ffn_gain)
    ffn_low = ffn_normed.astype(bf16)
    ffn_all = gather_rows(ffn_low)
    cot_all = gather_rows(cotangent.reshape(tok_rows, width))

    def route(rows, hits, live):
        logits = jnp.dot(rows, router_weight, preferred_element_type=f32)
        probs = jax.nn.softmax(logits, axis=-1)
        picked = hits * probs
        total = jnp.sum(picked, axis=-1, keepdims=True)
        return probs, picked, total, live[:, None] * picked / total

    router_probs, picked, picked_total, _ = route(ffn_low, chosen, valid_rows)
    gates_all = route(ffn_all, chosen_all, valid_all)[3]
    gates = lax.dynamic_slice_in_dim(gates_all, member * experts_here, experts_here, 1)
    prob_sums = jnp.sum(valid_rows[:, None] * router_probs, axis=0)

    out_grad_all = cot_all.astype(f32) * valid_all[:, None]
    gate_up = jnp.einsum("td,edf->etf", ffn_all, expert_in, preferred_element_type=f32)
    gate_pre = gate_up[..., :FF]
    up_pre = gate_up[..., FF:]
    gate_sigmoid = jax.nn.sigmoid(gate_pre)
    hidden = (gate_pre * gate_sigmoid * up_pre).astype(bf16)
    result = jnp.einsum("etf,efd->etd", hidden, expert_out, preferred_element_type=f32).astype(bf16)
    result_full = result.astype(f32)
    mixture = scatter_rows(
        jnp.sum(gates.T[:, :, None] * result_full, axis=0).astype(bf16)
    ).astype(f32)
    block_out = (residual + mixture).reshape(1, slot_count, seq_count, width)
    gate_grads_here = jnp.sum(result_full * out_grad_all[None], axis=-1).T
    gate_grads = (
        lax.all_to_all(
            gate_grads_here.reshape(n_expert, tok_rows, experts_here),
            "expert",
            split_axis=0,
            concat_axis=0,
            tiled=True,
        )
        .transpose(1, 0, 2)
        .reshape(tok_rows, experts_all)
        * chosen
    )
    pair_grad = (gates.T[:, :, None] * out_grad_all[None]).astype(bf16)
    hidden_grad = jnp.einsum("etd,efd->etf", pair_grad, expert_out, preferred_element_type=f32)
    gate_up_grad = jnp.concatenate(
        [
            hidden_grad * up_pre * gate_sigmoid * (1.0 + gate_pre * (1.0 - gate_sigmoid)),
            hidden_grad * gate_pre * gate_sigmoid,
        ],
        axis=-1,
    ).astype(bf16)
    pair_in = jnp.einsum("etf,edf->td", gate_up_grad, expert_in, preferred_element_type=f32)
    ffn_grad = scatter_rows(pair_in.astype(bf16)).astype(f32)
    in_terms = jnp.einsum("td,etf->edf", ffn_all, gate_up_grad, preferred_element_type=f32)
    out_terms = jnp.einsum("etf,etd->efd", hidden, pair_grad, preferred_element_type=f32)
    grad_expert_in = lax.psum_scatter(
        in_terms.astype(bf16), "dp", scatter_dimension=1, tiled=True
    ).astype(f32)
    grad_expert_out = lax.psum_scatter(
        out_terms.astype(bf16), "dp", scatter_dimension=1, tiled=True
    ).astype(f32)

    live = valid_rows[:, None]
    picked_grad = (
        live
        * chosen
        * (
            gate_grads / picked_total
            - jnp.sum(gate_grads * picked, axis=-1, keepdims=True) / (picked_total * picked_total)
        )
    )
    prob_grad = picked_grad + balance_coef * experts_all * fraction[None, :] / n_valid * live
    logit_grad = router_probs * (
        prob_grad - jnp.sum(router_probs * prob_grad, axis=-1, keepdims=True)
    )
    ffn_grad = ffn_grad + jnp.dot(logit_grad, router_weight.astype(f32).T, precision=PRECISE)
    router_terms = jnp.dot(ffn_low.astype(f32).T, logit_grad, precision=PRECISE)
    residual_norm_grad, ffn_gain_terms = ffn_back(ffn_grad)
    out_grad = cotangent.astype(f32).reshape(tok_rows, width) * live
    residual_grad = out_grad + residual_norm_grad
    branch_grad = residual_grad.astype(bf16)

    attended_grad = (
        lax.all_to_all(
            lax.dot_general(
                branch_grad, w_out, (((1,), (1,)), ((), ())), preferred_element_type=f32
            )
            .astype(bf16)
            .reshape(tok_rows, n_expert, cols),
            "expert",
            split_axis=1,
            concat_axis=0,
            tiled=True,
        )
    ).reshape(head_shape)
    probs_back = jnp.exp(scores_of() - log_total)
    prob_back = jnp.einsum("tshd,ushd->shtu", attended_grad, values, preferred_element_type=f32)
    row_dot = jnp.sum(probs_back * prob_back, axis=-1, keepdims=True)
    score_grad = (probs_back * (prob_back - row_dot)).astype(bf16)
    query_grad = (
        jnp.einsum("shtu,ushd->tshd", score_grad, key_rows, preferred_element_type=f32) * scale
    )
    key_grad = (
        jnp.einsum("shtu,tshd->ushd", score_grad, queries, preferred_element_type=f32) * scale
    )
    value_grad = jnp.einsum(
        "shtu,tshd->ushd", probs_back.astype(bf16), attended_grad, preferred_element_type=f32
    )
    query_proj_grad, key_proj_grad, q_gain_terms, k_gain_terms = heads_back((query_grad, key_grad))
    proj_grad = jnp.concatenate(
        [query_proj_grad, key_proj_grad, value_grad.reshape(all_rows, cols)], axis=1
    ).astype(bf16)
    normed_grad = scatter_rows(
        lax.dot_general(
            proj_grad, w_qkv, (((1,), (1,)), ((), ())), preferred_element_type=f32
        ).astype(bf16)
    ).astype(f32)
    input_norm_grad, attn_gain_terms = norm_back(normed_grad)
    grad_tokens = (residual_grad + input_norm_grad).reshape(1, slot_count, seq_count, width)

    proj_terms = lax.dot_general(
        normed_all, proj_grad, (((0,), (0,)), ((), ())), preferred_element_type=f32
    )
    proj_share = lax.psum_scatter(proj_terms.astype(bf16), "dp", scatter_dimension=0, tiled=True)
    grad_qkv = (
        lax.all_to_all(
            proj_share.reshape(n_expert, row_count, 3, cols),
            "expert",
            split_axis=0,
            concat_axis=0,
            tiled=True,
        )
        .transpose(1, 2, 0, 3)
        .reshape(row_count, 3, width)
        .astype(f32)
    )
    output_terms = lax.dot_general(
        attended_low, branch_grad, (((0,), (0,)), ((), ())), preferred_element_type=f32
    )
    grad_out = lax.psum_scatter(
        lax.psum_scatter(output_terms.astype(bf16), "dp", scatter_dimension=0, tiled=True),
        "expert",
        scatter_dimension=0,
        tiled=True,
    ).astype(f32)
    grad_attn_gain, grad_q_gain, grad_k_gain, grad_ffn_gain, grad_router, prob_total = lax.psum(
        (
            attn_gain_terms,
            q_gain_terms,
            k_gain_terms,
            ffn_gain_terms,
            router_terms,
            prob_sums,
        ),
        ("dp", "expert"),
    )
    balance_loss = balance_coef * experts_all * jnp.sum(fraction * (prob_total / n_valid))
    return (
        block_out,
        balance_loss,
        grad_tokens,
        grad_attn_gain,
        grad_q_gain,
        grad_k_gain,
        grad_qkv,
        grad_out,
        grad_ffn_gain,
        grad_router,
        grad_expert_in,
        grad_expert_out,
    )


def solution(mesh):
    placed = (
        P("dp", "expert", None, None),
        P(),
        P("dp", "expert", None, None),
        P(),
        P(),
        P(),
        P(("dp", "expert"), None, None),
        P(("dp", "expert"), None),
        P(),
        P(),
        P("expert", None, None),
        P("expert", None, None),
        P(),
        P("dp", "expert", None, None),
    )
    return jax.shard_map(
        body,
        mesh=mesh,
        in_specs=placed,
        out_specs=(
            P("dp", "expert", None, None),
            P(),
            P("dp", "expert", None, None),
            P(),
            P(),
            P(),
            P(("dp", "expert"), None, None),
            P(("dp", "expert"), None),
            P(),
            P(),
            P("expert", "dp", None),
            P("expert", "dp", None),
        ),
        check_vma=False,
    )
```

```python
import functools
import math

import jax
import jax.numpy as jnp
from jax import lax
from jax.experimental import pallas as pl
from jax.experimental.pallas import tpu as pltpu
from jax.sharding import PartitionSpec as P

HEADS = 16
HD = 128
FF = 1024
TOPK = 8


NORM_EPS = 1e-05
PRECISE = lax.Precision.HIGHEST


def norm_rows(values, scale_gain):
    return (
        values
        * lax.rsqrt(jnp.mean(values * values, axis=-1, keepdims=True) + NORM_EPS)
        * scale_gain
    )


VMEM_BYTES = 56 * 1024 * 1024
TILE = 256
WIDE = 512


def params():
    return pltpu.CompilerParams(vmem_limit_bytes=VMEM_BYTES)


def dot_nn(left, right):
    return jnp.dot(left, right, preferred_element_type=jnp.float32)


def dot_nt(left, right):
    return lax.dot_general(
        left, right, (((1,), (1,)), ((), ())), preferred_element_type=jnp.float32
    )


def dot_tn(left, right):
    return lax.dot_general(
        left, right, (((0,), (0,)), ((), ())), preferred_element_type=jnp.float32
    )


def turn(values, cosine, sine):
    return values * cosine + pltpu.roll(values, HD // 2, 1) * sine


def turn_back(values, cosine, sine):
    return values * cosine + pltpu.roll(values * sine, HD // 2, 1)


def head_norm(proj):
    return lax.rsqrt(jnp.mean(proj * proj, axis=-1, keepdims=True) + NORM_EPS)


def load_heads(proj_ref, cos_ref, sin_ref, gain_ref):
    rows = cos_ref.shape[0]
    proj = proj_ref[...].reshape(rows, 3 * HD)
    cosine, sine = cos_ref[...], sin_ref[...]
    q_proj, k_proj, v_proj = proj[:, :HD], proj[:, HD : 2 * HD], proj[:, 2 * HD :]
    queries = turn(q_proj * head_norm(q_proj) * gain_ref[0:1], cosine, sine).astype(jnp.bfloat16)
    keys = turn(k_proj * head_norm(k_proj) * gain_ref[1:2], cosine, sine).astype(jnp.bfloat16)
    return q_proj, k_proj, queries, keys, v_proj.astype(jnp.bfloat16)


def row_probs(queries, keys, live):
    scores = jnp.where(live, dot_nt(queries, keys), -1e30)
    expo = jnp.exp((scores - jnp.max(scores, axis=-1, keepdims=True)) * (1.0 / math.sqrt(HD)))
    return expo * (1.0 / jnp.sum(expo, axis=-1, keepdims=True))


def attend_kernel(
    owner_ref, proj_ref, cos_ref, sin_ref, live_ref, gain_ref, out_ref, q_scr, o_scr
):
    rows, slots = cos_ref.shape[0], proj_ref.shape[2]
    step = min(TILE, rows)
    _, _, queries, keys, values = load_heads(proj_ref, cos_ref, sin_ref, gain_ref)
    q_scr[...] = queries
    live = live_ref[0] > 0.0

    def chunk(i, carry):
        part = pl.ds(pl.multiple_of(i * step, step), step)
        probs = row_probs(q_scr[part, :], keys, live).astype(jnp.bfloat16)
        o_scr[part, :] = dot_nn(probs, values).astype(jnp.bfloat16)
        return carry

    lax.fori_loop(0, rows // step, chunk, 0, unroll=True)
    for r in range(proj_ref.shape[0]):
        out_ref[owner_ref[r], 0] = o_scr[r * slots : (r + 1) * slots, :]


def attend(owners, proj, cosine, sine, live, gains):
    blocks, seqs, slots, width = proj.shape
    heads, rows = width // (3 * HD), blocks * slots
    return pl.pallas_call(
        attend_kernel,
        grid_spec=pltpu.PrefetchScalarGridSpec(
            num_scalar_prefetch=1,
            grid=(seqs, heads),
            in_specs=[
                pl.BlockSpec((blocks, 1, slots, 3 * HD), lambda s, h, o: (0, s, 0, h)),
                pl.BlockSpec((rows, HD), lambda s, h, o: (0, 0)),
                pl.BlockSpec((rows, HD), lambda s, h, o: (0, 0)),
                pl.BlockSpec((1, 1, rows), lambda s, h, o: (s, 0, 0)),
                pl.BlockSpec((2, HD), lambda s, h, o: (0, 0)),
            ],
            out_specs=pl.BlockSpec((blocks, 1, slots, HD), lambda s, h, o: (0, s, 0, h)),
            scratch_shapes=[pltpu.VMEM((rows, HD), jnp.bfloat16)] * 2,
        ),
        out_shape=jax.ShapeDtypeStruct((blocks, seqs, slots, heads * HD), jnp.bfloat16),
        compiler_params=params(),
        cost_estimate=pl.CostEstimate(
            flops=4 * seqs * heads * rows * rows * HD,
            bytes_accessed=seqs * rows * width * 5,
            transcendentals=seqs * heads * rows * rows,
        ),
        name="attend",
    )(owners, proj, cosine, sine, live, gains)


def attend_back_kernel(
    owner_ref, proj_ref, grad_ref, cos_ref, sin_ref, live_ref, gain_ref, out_ref, gain_out, q_scr, dq, dk, dv
):
    rows, slots = cos_ref.shape[0], proj_ref.shape[2]
    step = min(TILE, rows)
    scale = 1.0 / math.sqrt(HD)
    q_proj, k_proj, queries, keys, values = load_heads(proj_ref, cos_ref, sin_ref, gain_ref)
    q_scr[0] = queries
    for r in range(proj_ref.shape[0]):
        q_scr[1, r * slots : (r + 1) * slots, :] = grad_ref[owner_ref[r], 0]
    dk[...] = jnp.zeros_like(dk)
    dv[...] = jnp.zeros_like(dv)
    live = live_ref[0] > 0.0

    def chunk(i, carry):
        part = pl.ds(pl.multiple_of(i * step, step), step)
        q_part, g_part = q_scr[0, part, :], q_scr[1, part, :]
        probs = row_probs(q_part, keys, live)
        prob_grad = dot_nt(g_part, values)
        row_dot = jnp.sum(probs * prob_grad, axis=-1, keepdims=True)
        score_grad = (probs * (prob_grad - row_dot)).astype(jnp.bfloat16)
        dq[part, :] = dot_nn(score_grad, keys)
        dk[...] += dot_tn(score_grad, q_part)
        dv[...] += dot_tn(probs.astype(jnp.bfloat16), g_part)
        return carry

    lax.fori_loop(0, rows // step, chunk, 0, unroll=True)
    cosine, sine = cos_ref[...], sin_ref[...]
    parts = []
    for i, (proj, grad) in enumerate(((q_proj, dq), (k_proj, dk))):
        gain, inverse = gain_ref[i : i + 1], head_norm(proj)
        back = turn_back(grad[...] * scale, cosine, sine)
        scaled = proj * inverse
        gain_out[0, 0, i : i + 1, :] = jnp.sum(back * scaled, axis=0, keepdims=True)
        back = back * gain
        parts.append(
            inverse * (back - scaled * jnp.mean(scaled * back, axis=-1, keepdims=True))
        )
    grads = jnp.concatenate(parts + [dv[...]], axis=1).astype(jnp.bfloat16)
    out_ref[...] = grads.reshape(out_ref.shape)


def attend_back(owners, proj, grads, cosine, sine, live, gains):
    blocks, seqs, slots, width = proj.shape
    heads, rows = width // (3 * HD), blocks * slots
    return pl.pallas_call(
        attend_back_kernel,
        grid_spec=pltpu.PrefetchScalarGridSpec(
            num_scalar_prefetch=1,
            grid=(seqs, heads),
            in_specs=[
                pl.BlockSpec((blocks, 1, slots, 3 * HD), lambda s, h, o: (0, s, 0, h)),
                pl.BlockSpec((blocks, 1, slots, HD), lambda s, h, o: (0, s, 0, h)),
                pl.BlockSpec((rows, HD), lambda s, h, o: (0, 0)),
                pl.BlockSpec((rows, HD), lambda s, h, o: (0, 0)),
                pl.BlockSpec((1, 1, rows), lambda s, h, o: (s, 0, 0)),
                pl.BlockSpec((2, HD), lambda s, h, o: (0, 0)),
            ],
            out_specs=[
                pl.BlockSpec((blocks, 1, slots, 3 * HD), lambda s, h, o: (0, s, 0, h)),
                pl.BlockSpec((1, 1, 2, HD), lambda s, h, o: (s, h, 0, 0)),
            ],
            scratch_shapes=[pltpu.VMEM((2, rows, HD), jnp.bfloat16)]
            + [pltpu.VMEM((rows, HD), jnp.float32)] * 3,
        ),
        out_shape=[
            jax.ShapeDtypeStruct(proj.shape, jnp.bfloat16),
            jax.ShapeDtypeStruct((seqs, heads, 2, HD), jnp.float32),
        ],
        compiler_params=params(),
        cost_estimate=pl.CostEstimate(
            flops=10 * seqs * heads * rows * rows * HD,
            bytes_accessed=seqs * rows * width * 7,
            transcendentals=seqs * heads * rows * rows,
        ),
        name="attend_back",
    )(owners, proj, grads, cosine, sine, live, gains)


def gate_column(gates_ref, index):
    gates = gates_ref[...]
    out = jnp.zeros((gates.shape[0], 1), jnp.float32)
    for e in range(gates.shape[1]):
        out = out + jnp.where(index == e, gates[:, e : e + 1], 0.0)
    return out


def fill_rows(refs, out_ref):
    base = 0
    for ref in refs:
        out_ref[base : base + ref.shape[0], :] = ref[...]
        base += ref.shape[0]


def experts_kernel(parts, held, tiles, per, count, *refs):
    x_refs, refs = refs[:parts], refs[parts:]
    hits_ref, router_ref, own_ref, gate_w, up_w, down_w = refs[:6]
    rows, gate_out, up_out, gated_out, gates_ref, mix_out, gated = refs[6 + held :]
    i = pl.program_id(0)

    @pl.when(i == 0)
    def _():
        fill_rows(x_refs, rows)
        logits = dot_nn(rows[...], router_ref[...])
        hits = hits_ref[...]
        lane = lax.broadcasted_iota(jnp.int32, logits.shape, 1)
        logits = jnp.where(lane < count, logits, -1e30)
        expo = jnp.exp(logits - jnp.max(logits, axis=1, keepdims=True))
        picked = jnp.where(lane < count, hits * expo / jnp.sum(expo, axis=1, keepdims=True), 0.0)
        live = jnp.sum(jnp.where(lane == count, hits, 0.0), axis=1, keepdims=True)
        gates = live * picked / jnp.sum(picked, axis=1, keepdims=True)
        for e in range(gates_ref.shape[1]):
            gates_ref[:, e : e + 1] = jnp.sum(gates * own_ref[e : e + 1], axis=1, keepdims=True)

    @pl.when(i < tiles)
    def _():
        gate = dot_nn(rows[...], gate_w[0])
        up = dot_nn(rows[...], up_w[0])
        hidden = gate / (1.0 + jnp.exp(-gate)) * up * gate_column(gates_ref, i // per)
        gate_out[...] = gate.astype(jnp.bfloat16)
        up_out[...] = up.astype(jnp.bfloat16)
        low = hidden.astype(jnp.bfloat16)
        gated_out[...] = low
        gated[:, pl.ds(pl.multiple_of(i * WIDE, WIDE), WIDE)] = low

    @pl.when(i >= tiles)
    def _():
        mix_out[...] = dot_nn(gated[...], down_w[...]).astype(jnp.bfloat16)


def experts_forward(xs, hits, router, own, count, w_in, w_down, held, base, total):
    experts, width, _ = w_in.shape
    hidden = w_down.shape[0]
    rows = sum(x.shape[0] for x in xs)
    place = base // rows
    tiles, per, outs = hidden // WIDE, FF // WIDE, width // WIDE
    clamp = lambda i: jnp.minimum(i, tiles - 1)
    later = lambda i: jnp.maximum(i - tiles, 0)
    keep = pl.BlockSpec((rows, WIDE), lambda i: (place, clamp(i)))
    known = len(xs) + 6
    lanes = router.shape[1]
    return pl.pallas_call(
        functools.partial(experts_kernel, len(xs), len(held), tiles, per, count),
        grid=(tiles + outs,),
        in_specs=[pl.BlockSpec(x.shape, lambda i: (0, 0)) for x in xs]
        + [
            pl.BlockSpec((rows, lanes), lambda i: (0, 0)),
            pl.BlockSpec((width, lanes), lambda i: (0, 0)),
            pl.BlockSpec((experts, lanes), lambda i: (0, 0)),
            pl.BlockSpec((1, width, WIDE), lambda i: (clamp(i) // per, 0, clamp(i) % per)),
            pl.BlockSpec((1, width, WIDE), lambda i: (clamp(i) // per, 0, per + clamp(i) % per)),
            pl.BlockSpec((hidden, WIDE), lambda i: (0, later(i))),
        ]
        + [pl.BlockSpec(memory_space=pl.ANY)] * len(held),
        out_specs=[pl.BlockSpec((rows, width), lambda i: (place, 0))]
        + [keep] * 3
        + [
            pl.BlockSpec((rows, experts), lambda i: (0, 0)),
            pl.BlockSpec((rows, WIDE), lambda i: (0, later(i))),
        ],
        out_shape=[jax.ShapeDtypeStruct((total, width), jnp.bfloat16)]
        + [jax.ShapeDtypeStruct((total, hidden), jnp.bfloat16)] * 3
        + [
            jax.ShapeDtypeStruct((rows, experts), jnp.float32),
            jax.ShapeDtypeStruct((rows, width), jnp.bfloat16),
        ],
        scratch_shapes=[pltpu.VMEM((rows, hidden), jnp.bfloat16)],
        input_output_aliases={known + i: i for i in range(len(held))},
        compiler_params=params(),
        cost_estimate=pl.CostEstimate(
            flops=6 * rows * hidden * width,
            bytes_accessed=6 * hidden * width + 10 * rows * width,
            transcendentals=rows * hidden,
        ),
        name="experts_forward",
    )(*xs, hits, router, own, w_in, w_in, w_down, *held)


def experts_back_kernel(parts, held, tiles, per, *refs):
    c_refs, refs = refs[:parts], refs[parts:]
    gates_ref, own_ref, gate_ref, up_ref, down_w, in_w = refs[:6]
    rows, gate_out, up_out, score_out, grad_out, gate_grads, up_grads = refs[6 + held :]
    i = pl.program_id(0)

    @pl.when(i == 0)
    def _():
        fill_rows(c_refs, rows)

    @pl.when(i < tiles)
    def _():
        raw = dot_nt(rows[...], down_w[...])
        gate, up = gate_ref[...].astype(jnp.float32), up_ref[...].astype(jnp.float32)
        sigmoid = 1.0 / (1.0 + jnp.exp(-gate))
        silu = gate * sigmoid
        score = jnp.sum(silu * up * raw, axis=1, keepdims=True)
        own = own_ref[...]
        place = sum(jnp.where(i // per == e, own[e : e + 1], 0.0) for e in range(own.shape[0]))
        mine = score * place
        score_out[...] = jnp.where(i == 0, mine, score_out[...] + mine)
        grad = raw * gate_column(gates_ref, i // per)
        gate_low = (grad * up * (sigmoid + silu * (1.0 - sigmoid))).astype(jnp.bfloat16)
        up_low = (grad * silu).astype(jnp.bfloat16)
        gate_out[...] = gate_low
        up_out[...] = up_low
        part = pl.ds(pl.multiple_of(i * WIDE, WIDE), WIDE)
        gate_grads[:, part] = gate_low
        up_grads[:, part] = up_low

    @pl.when(i >= tiles)
    def _():
        total = 0.0
        for e in range(in_w.shape[0]):
            part = slice(e * FF, (e + 1) * FF)
            total = total + dot_nt(gate_grads[:, part], in_w[e, :, :FF])
            total = total + dot_nt(up_grads[:, part], in_w[e, :, FF:])
        grad_out[...] = total.astype(jnp.bfloat16)


def experts_backward(outs, gates, own, gate, up, w_in, w_down, held, base):
    experts, width, _ = w_in.shape
    hidden, total = w_down.shape[0], gate.shape[0]
    rows = sum(o.shape[0] for o in outs)
    place = base // rows
    tiles, per, last = hidden // WIDE, FF // WIDE, width // WIDE
    clamp = lambda i: jnp.minimum(i, tiles - 1)
    later = lambda i: jnp.maximum(i - tiles, 0)
    keep = pl.BlockSpec((rows, WIDE), lambda i: (place, clamp(i)))
    known, lanes = len(outs) + 6, own.shape[1]
    return pl.pallas_call(
        functools.partial(experts_back_kernel, len(outs), len(held), tiles, per),
        grid=(tiles + last,),
        in_specs=[pl.BlockSpec(o.shape, lambda i: (0, 0)) for o in outs]
        + [
            pl.BlockSpec((rows, experts), lambda i: (0, 0)),
            pl.BlockSpec((experts, lanes), lambda i: (0, 0)),
            keep,
            keep,
            pl.BlockSpec((WIDE, width), lambda i: (clamp(i), 0)),
            pl.BlockSpec((experts, WIDE, 2 * FF), lambda i: (0, later(i), 0)),
        ]
        + [pl.BlockSpec(memory_space=pl.ANY)] * len(held),
        out_specs=[
            pl.BlockSpec((rows, width), lambda i: (place, 0)),
            keep,
            keep,
            pl.BlockSpec((rows, lanes), lambda i: (0, 0)),
            pl.BlockSpec((rows, WIDE), lambda i: (0, later(i))),
        ],
        out_shape=[jax.ShapeDtypeStruct((total, width), jnp.bfloat16)]
        + [jax.ShapeDtypeStruct((total, hidden), jnp.bfloat16)] * 2
        + [
            jax.ShapeDtypeStruct((rows, lanes), jnp.float32),
            jax.ShapeDtypeStruct((rows, width), jnp.bfloat16),
        ],
        scratch_shapes=[pltpu.VMEM((rows, hidden), jnp.bfloat16)] * 2,
        input_output_aliases={known + i: i for i in range(len(held))},
        compiler_params=params(),
        cost_estimate=pl.CostEstimate(
            flops=6 * rows * hidden * width,
            bytes_accessed=6 * hidden * width + 12 * rows * width,
            transcendentals=rows * hidden,
        ),
        name="experts_backward",
    )(*outs, gates, own, gate, up, w_down, w_in, *held)


def ring_order(size):
    return list(range(0, size, 2)) + list(range(size - 1, 0, -2))


def ring_shift(rows, order, step):
    size = len(order)
    pairs = [(order[i], order[(i + step) % size]) for i in range(size)]
    return lax.ppermute(rows, "expert", pairs)


class Gather:
    def __init__(self, rows, order):
        self.order, self.half, self.done = order, len(order) // 2, 0
        self.blocks = {0: rows}

    def step(self, *waits):
        self.done = s = self.done + 1
        ahead, back = self.blocks[1 - s], self.blocks[s - 1]
        if s == self.half:
            cut = ahead.shape[0] // 2
            ahead, back = ahead[:cut], back[cut:]
        if waits:
            ahead, back = lax.optimization_barrier((ahead, back, *waits))[:2]
        ahead, back = ring_shift(ahead, self.order, 1), ring_shift(back, self.order, -1)
        if s == self.half:
            self.blocks[s] = jnp.concatenate([ahead, back], axis=0)
        else:
            self.blocks[-s], self.blocks[s] = ahead, back


class Scatter:
    def __init__(self, far, order, *waits):
        self.order, self.cut, self.first = order, far.shape[0] // 2, True
        self.send(far[: self.cut], far[self.cut :], waits)

    def send(self, ahead, back, waits):
        ahead, back = ahead.astype(jnp.bfloat16), back.astype(jnp.bfloat16)
        if waits:
            ahead, back = lax.optimization_barrier((ahead, back, *waits))[:2]
        self.ahead = ring_shift(ahead, self.order, 1).astype(jnp.float32)
        self.back = ring_shift(back, self.order, -1).astype(jnp.float32)

    def step(self, mine, other, *waits):
        mine, other = mine.astype(jnp.float32), other.astype(jnp.float32)
        if self.first:
            cut, self.first = self.cut, False
            mine = jnp.concatenate([mine[:cut] + self.ahead, mine[cut:]], axis=0)
            other = jnp.concatenate([other[:cut], other[cut:] + self.back], axis=0)
        else:
            mine, other = mine + self.ahead, other + self.back
        self.send(mine, other, waits)

    def finish(self, own):
        return own.astype(jnp.float32) + self.ahead + self.back


def offsets_of(size):
    half = size // 2
    out = [0]
    for step in range(1, half):
        out += [-step, step]
    return out + [half]


def sum_over(values, axis):
    size, step = lax.axis_size(axis), 1
    while step < size:
        values = values + lax.ppermute(values, axis, [(i, i ^ step) for i in range(size)])
        step *= 2
    return values


def gather_small(rows, axis):
    size, step, me = lax.axis_size(axis), 1, lax.axis_index(axis)
    while step < size:
        other = lax.ppermute(rows, axis, [(i, i ^ step) for i in range(size)])
        upper = (me // step) % 2 == 1
        rows = jnp.concatenate(
            [jnp.where(upper, other, rows), jnp.where(upper, rows, other)], axis=0
        )
        step *= 2
    return rows


def after(values, *others):
    return lax.optimization_barrier((values, *others))[0]


def weight_kernel(parts, adds, index_ref, *refs):
    left_refs, right_ref, refs = refs[:parts], refs[parts], refs[parts + 1 :]
    add_refs, out_ref, left = refs[: adds * parts], refs[-2], refs[-1]
    tile = left_refs[0].shape[1]

    @pl.when(pl.program_id(0) == 0)
    def _():
        for p, ref in enumerate(left_refs):
            left[p * tile : (p + 1) * tile, :] = ref[...].T

    total = dot_nn(left[...], right_ref[...])
    for p in range(parts):
        part = total[p * tile : (p + 1) * tile]
        for a in range(adds):
            part = part + add_refs[a * parts + p][...].astype(jnp.float32)
        out_ref[p * tile : (p + 1) * tile, :] = part.astype(out_ref.dtype)


def weight_part(left, right, tile, columns, adds, dtype, name):
    rows, width, wide = left.shape[0], right.shape[1], WIDE
    parts = len(columns)
    places = list(columns) + [t for _, tiles in adds for t in tiles]
    in_specs = [
        pl.BlockSpec((rows, tile), lambda j, at, p=p: (0, at[p])) for p in range(parts)
    ] + [pl.BlockSpec((rows, wide), lambda j, at: (0, j))]
    in_specs += [
        pl.BlockSpec((tile, wide), lambda j, at, p=p: (at[p], j))
        for p in range(parts, len(places))
    ]
    return pl.pallas_call(
        functools.partial(weight_kernel, parts, len(adds)),
        grid_spec=pltpu.PrefetchScalarGridSpec(
            num_scalar_prefetch=1,
            grid=(width // wide,),
            in_specs=in_specs,
            out_specs=pl.BlockSpec((parts * tile, wide), lambda j, at: (0, j)),
            scratch_shapes=[pltpu.VMEM((parts * tile, rows), jnp.bfloat16)],
        ),
        out_shape=jax.ShapeDtypeStruct((parts * tile, width), dtype),
        compiler_params=params(),
        cost_estimate=pl.CostEstimate(
            flops=2 * rows * parts * tile * width,
            bytes_accessed=2 * rows * (parts * tile + width) + 4 * parts * tile * width,
            transcendentals=0,
        ),
        name=name,
    )(
        jnp.stack([jnp.asarray(p, jnp.int32) for p in places]),
        *[left] * parts,
        right,
        *[a for a, tiles in adds for _ in tiles],
    )


class GroupSum:
    def __init__(self, left, right, outer, name):
        self.left, self.right, self.outer, self.name = left, right, outer, name
        self.size = lax.axis_size("dp")
        me = lax.axis_index("dp")
        self.core, self.pair = me % 2, me // 2
        self.tile = left.shape[1] // outer // self.size

    def tiles(self, core, pairs):
        return [4 * o + 2 * pair + core for o in range(self.outer) for pair in pairs]

    def part(self, columns, adds, dtype, waits):
        left = after(self.left, *waits) if waits else self.left
        return weight_part(left, self.right, self.tile, columns, adds, dtype, self.name)

    def first(self, *waits):
        if self.size != 4:
            left = after(self.left, *waits) if waits else self.left
            terms = dot_tn(left, self.right).astype(jnp.bfloat16)
            terms = terms.reshape(self.outer, -1, terms.shape[1])
            self.far = lax.psum_scatter(terms, "dp", scatter_dimension=1, tiled=True)
            return
        columns = self.tiles(1 - self.core, (0, 1))
        self.far = self.part(columns, [], jnp.bfloat16, waits)
        self.got = lax.ppermute(self.far, "dp", [(i, i ^ 1) for i in range(4)])

    def halves(self, pair):
        return [2 * o + pair for o in range(self.outer)]

    def second(self, *waits):
        if self.size != 4:
            return
        other = 1 - self.pair
        terms = self.part(
            self.tiles(self.core, (other,)),
            [(self.got, self.halves(other))],
            jnp.bfloat16,
            waits,
        )
        self.near = lax.ppermute(terms, "dp", [(i, i ^ 2) for i in range(4)])

    def third(self, *waits):
        if self.size != 4:
            return self.far.reshape(-1, self.far.shape[-1]).astype(jnp.float32)
        return self.part(
            self.tiles(self.core, (self.pair,)),
            [(self.got, self.halves(self.pair)), (self.near, range(self.outer))],
            jnp.float32,
            waits,
        )


def body(
    tokens,
    lengths,
    routes,
    attn_gain,
    q_gain,
    k_gain,
    qkv_weight,
    out_weight,
    ffn_gain,
    router_weight,
    expert_in,
    expert_out,
    balance_coef,
    cotangent,
):
    bf16, f32 = jnp.bfloat16, jnp.float32
    n_expert = lax.axis_size("expert")
    group_index = lax.axis_index("dp")
    member = lax.axis_index("expert")
    slot_count = tokens.shape[1]
    seq_count = tokens.shape[2]
    width = tokens.shape[3]
    experts_here = expert_in.shape[0]
    experts_all = experts_here * n_expert
    tok_rows = slot_count * seq_count
    full_len = slot_count * n_expert
    heads_here = HEADS // n_expert
    cols = heads_here * HD

    order = ring_order(n_expert)
    offsets = offsets_of(n_expert)
    half = n_expert // 2
    table = [[order[(order.index(m) + r) % n_expert] for r in offsets] for m in range(n_expert)]
    owners = lax.dynamic_index_in_dim(jnp.array(table, jnp.int32), member, 0, False)
    owner = {r: owners[i] for i, r in enumerate(offsets)}

    def blockwise(blocks, axis=0):
        return jnp.concatenate([blocks[r] for r in offsets], axis=axis)

    def to_rows(values):
        return jnp.swapaxes(values[0], 0, 1).reshape(tok_rows, values.shape[3])

    def from_rows(rows):
        return jnp.swapaxes(rows.reshape(seq_count, slot_count, width), 0, 1)[None]

    seq_lens = lengths[group_index]
    slot_ids = member * slot_count + jnp.arange(slot_count)
    valid_rows = (slot_ids[None, :] < seq_lens[:, None]).astype(f32).reshape(tok_rows)
    all_slots = (owners[:, None] * slot_count + jnp.arange(slot_count)[None, :]).reshape(full_len)
    key_live = (all_slots[None, :] < seq_lens[:, None]).astype(f32)[:, None, :]
    inv_freq = jnp.exp(
        jnp.arange(HD // 2, dtype=f32) * (-2.0 * math.log(10000.0) / HD)
    )
    angles = all_slots.astype(f32)[:, None] * inv_freq[None, :]
    cosine, sine = jnp.cos(angles), jnp.sin(angles)
    cosine = jnp.concatenate([cosine, cosine], axis=1)
    sine = jnp.concatenate([-sine, sine], axis=1)
    head_gains = jnp.stack([q_gain, k_gain])

    inputs = to_rows(tokens).astype(f32)
    normed = norm_rows(inputs, attn_gain)
    normed_ring = Gather(normed.astype(bf16), order)
    normed_ring.step()

    row_count = qkv_weight.shape[0]
    w_cols = qkv_weight.reshape(row_count, 3, n_expert, heads_here, HD).transpose(2, 0, 3, 1, 4)
    w_cols = lax.all_to_all(
        after(w_cols.reshape(n_expert, row_count, 3 * cols), normed_ring.blocks[1]),
        "expert",
        split_axis=0,
        concat_axis=0,
        tiled=True,
    )
    w_qkv = lax.all_gather(w_cols.reshape(-1, 3 * cols), "dp", axis=0, tiled=True)
    w_out = lax.all_gather(out_weight, "expert", axis=0, tiled=True)
    for _ in range(half - 1):
        normed_ring.step()
    normed_all = blockwise(normed_ring.blocks)
    w_out = lax.all_gather(after(w_out, normed_all), "dp", axis=0, tiled=True)
    cot_rows = to_rows(cotangent)
    cot_ring = Gather(cot_rows, order)
    cot_ring.step(normed_all)

    picked_ids = to_rows(routes)
    chosen = jnp.sum(
        (picked_ids[:, :, None] == jnp.arange(experts_all)[None, None, :]).astype(f32), axis=1
    )
    lanes = 128
    hits = jnp.concatenate([chosen, valid_rows[:, None]], axis=1).T
    hits = jnp.pad(hits, ((0, -hits.shape[0] % 16), (0, 0))).astype(bf16)
    hits_all = gather_small(hits[None], "expert")
    hits_of = {
        r: jnp.pad(
            lax.dynamic_index_in_dim(hits_all, owner[r], 0, False).T.astype(f32),
            ((0, 0), (0, lanes - hits.shape[0])),
        )
        for r in offsets
    }
    router_pad = jnp.pad(router_weight, ((0, 0), (0, lanes - experts_all)))
    own_ids = member * experts_here + jnp.arange(experts_here)
    own_rows = (own_ids[:, None] == jnp.arange(lanes)[None, :]).astype(f32)
    n_valid = jnp.sum(lengths).astype(f32)
    count_total = sum_over(
        sum_over(jnp.sum(valid_rows[:, None] * chosen, axis=0), "expert"), "dp"
    )
    fraction = count_total / (TOPK * n_valid)

    project = dot_nn(normed_all, w_qkv).reshape(n_expert, seq_count, slot_count, 3 * cols)
    cot_ring.step(project)
    attended = attend(owners, project, cosine, sine, key_live, head_gains)
    attended_low = lax.all_to_all(
        attended.reshape(n_expert, tok_rows, cols), "expert", split_axis=0, concat_axis=0, tiled=True
    )
    attended_low = jnp.swapaxes(attended_low, 0, 1).reshape(tok_rows, width)
    for _ in range(half - 3):
        cot_ring.step(attended_low)
    residual = inputs + dot_nn(attended_low, w_out)
    ffn_normed, ffn_back = jax.vjp(norm_rows, residual, ffn_gain)
    ffn_low = ffn_normed.astype(bf16)
    ffn_ring = Gather(ffn_low, order)
    ffn_ring.step()

    live = valid_rows[:, None]
    router_probs = jax.nn.softmax(dot_nn(ffn_low, router_weight), axis=-1)
    picked = chosen * router_probs
    picked_total = jnp.sum(picked, axis=-1, keepdims=True)
    prob_sums = jnp.sum(live * router_probs, axis=0)
    groups = [[0]] + [[-s, s] for s in range(1, half)] + [[half]]
    bases = [(n_expert - 2) * tok_rows]
    bases += [2 * s * tok_rows for s in range(half - 1)] + [(n_expert - 1) * tok_rows]
    w_down = expert_out.reshape(experts_here * FF, width)
    all_rows = n_expert * tok_rows

    def split(rows, group):
        return {r: rows[i * tok_rows : (i + 1) * tok_rows] for i, r in enumerate(group)}

    held, mix_blocks, group_gates = [], {}, []
    for i, g in enumerate(groups):
        *held, gates, mixed = experts_forward(
            [ffn_ring.blocks[r] for r in g],
            jnp.concatenate([hits_of[r] for r in g], axis=0),
            router_pad,
            own_rows,
            experts_all,
            expert_in,
            w_down,
            held,
            bases[i],
            all_rows,
        )
        group_gates.append(gates)
        mix_blocks.update(split(mixed, g))
        if i < half - 1:
            ffn_ring.step(mixed)
        if i == 1:
            cot_ring.step(mixed)
    x_all, gate_all, up_all, gated_all = held
    held, ffn_sum = [], None
    for i in reversed(range(len(groups))):
        g = groups[i]
        *held, scores, grads = experts_backward(
            [cot_ring.blocks[r] for r in g],
            group_gates[i],
            own_rows,
            gate_all,
            up_all,
            expert_in,
            w_down,
            held,
            bases[i],
        )
        grads = jnp.concatenate([grads, scores.astype(bf16)], axis=1)
        if i == half:
            ffn_sum = Scatter(grads, order)
        elif i > 0:
            ffn_sum.step(grads[tok_rows:], grads[:tok_rows])
    out_all, gate_grad_all, up_grad_all = held
    ffn_grad = ffn_sum.finish(grads)
    gate_grads = ffn_grad[:, width : width + experts_all] * chosen
    ffn_grad = ffn_grad[:, :width]
    mix_sum = Scatter(mix_blocks[half], order, ffn_grad)
    picked_grad = (
        live
        * chosen
        * (
            gate_grads / picked_total
            - jnp.sum(gate_grads * picked, axis=-1, keepdims=True) / (picked_total * picked_total)
        )
    )
    prob_grad = picked_grad + balance_coef * experts_all * fraction[None, :] / n_valid * live
    logit_grad = router_probs * (
        prob_grad - jnp.sum(router_probs * prob_grad, axis=-1, keepdims=True)
    )
    ffn_grad = ffn_grad + jnp.dot(logit_grad, router_weight.astype(f32).T, precision=PRECISE)
    router_terms = jnp.dot(ffn_low.astype(f32).T, logit_grad, precision=PRECISE)
    residual_norm_grad, ffn_gain_terms = ffn_back(ffn_grad)
    residual_grad = cot_rows.astype(f32) * live + residual_norm_grad
    branch_grad = residual_grad.astype(bf16)

    attended_grad = dot_nt(branch_grad, w_out).astype(bf16)
    mix_sum.step(mix_blocks[half - 1], mix_blocks[1 - half], attended_grad)
    attended_grad = lax.all_to_all(
        jnp.swapaxes(attended_grad.reshape(tok_rows, n_expert, cols), 0, 1),
        "expert",
        split_axis=0,
        concat_axis=0,
        tiled=True,
    ).reshape(attended.shape)

    output_terms = dot_tn(attended_low, branch_grad).astype(bf16)
    grad_out = lax.psum_scatter(
        lax.psum_scatter(output_terms, "dp", scatter_dimension=0, tiled=True),
        "expert",
        scatter_dimension=0,
        tiled=True,
    ).astype(f32)
    sums = [
        GroupSum(gated_all, out_all, experts_here, "weights_out"),
        GroupSum(x_all, gate_grad_all, 1, "weights_gate"),
        GroupSum(x_all, up_grad_all, 1, "weights_up"),
    ]
    sums[0].first(branch_grad)
    attended_grad = after(attended_grad, sums[0].far)

    proj_grad, gain_parts = attend_back(
        owners, project, attended_grad, cosine, sine, key_live, head_gains
    )
    for s in range(half - 2, 0, -1):
        mix_sum.step(mix_blocks[s], mix_blocks[-s], proj_grad if s == 1 else attended_grad)
    proj_grad = proj_grad.reshape(all_rows, 3 * cols)
    normed_terms = dot_nt(proj_grad, w_qkv).astype(bf16)
    normed_parts = {
        r: normed_terms[i * tok_rows : (i + 1) * tok_rows] for i, r in enumerate(offsets)
    }
    normed_sum = Scatter(normed_parts[half], order)
    proj_terms = dot_tn(after(normed_all, normed_terms), proj_grad).astype(bf16)
    proj_share = lax.psum_scatter(proj_terms, "dp", scatter_dimension=0, tiled=True)
    sums[0].second(proj_terms)
    sums[1].first(proj_terms)
    for s in range(half - 1, 0, -1):
        normed_sum.step(normed_parts[s], normed_parts[-s])
        if s == half - 1:
            sums[2].first(normed_sum.ahead, sums[1].far)
            sums[1].second(sums[2].far)
        if s == half - 2:
            sums[2].second(normed_sum.ahead)
    normed_grad = normed_sum.finish(normed_parts[0])
    (input_norm_grad,) = jax.vjp(lambda v: norm_rows(v, attn_gain), inputs)[1](normed_grad)
    grad_tokens = from_rows(residual_grad + input_norm_grad)
    block_out = from_rows(residual + mix_sum.finish(mix_blocks[0]))
    grad_expert_out = sums[0].third(normed_sum.ahead).reshape(experts_here, -1, width)
    shares = [sums[1].third(normed_sum.ahead), sums[2].third(normed_sum.ahead)]
    grad_expert_in = jnp.stack(
        [
            jnp.concatenate([s[:, e * FF : (e + 1) * FF] for s in shares], axis=1)
            for e in range(experts_here)
        ]
    )

    grad_qkv = lax.all_to_all(
        proj_share.reshape(n_expert, row_count, 3 * cols),
        "expert",
        split_axis=0,
        concat_axis=0,
        tiled=True,
    ).reshape(n_expert, row_count, heads_here, 3, HD)
    grad_qkv = grad_qkv.transpose(1, 3, 0, 2, 4).reshape(row_count, 3, width).astype(f32)

    early = jnp.concatenate([router_terms.reshape(-1), ffn_gain_terms, prob_sums])
    early = sum_over(sum_over(early, "expert"), "dp")
    grad_router = early[: width * experts_all].reshape(width, experts_all)
    grad_ffn_gain = early[width * experts_all : width * experts_all + width]
    prob_total = early[width * experts_all + width :]
    head_gain_grads = jnp.sum(gain_parts, axis=(0, 1)).reshape(-1)
    attn_gain_terms = (
        jnp.sum(normed_terms.astype(f32) * normed_all.astype(f32), axis=0) / attn_gain
    )
    late = jnp.concatenate([attn_gain_terms, head_gain_grads])
    late = sum_over(sum_over(late, "expert"), "dp")
    balance_loss = balance_coef * experts_all * jnp.sum(fraction * (prob_total / n_valid))
    return (
        block_out,
        balance_loss,
        grad_tokens,
        late[:width],
        late[width : width + HD],
        late[width + HD :],
        grad_qkv,
        grad_out,
        grad_ffn_gain,
        grad_router,
        grad_expert_in,
        grad_expert_out,
    )


def solution(mesh):
    placed = (
        P("dp", "expert", None, None),
        P(),
        P("dp", "expert", None, None),
        P(),
        P(),
        P(),
        P(("dp", "expert"), None, None),
        P(("dp", "expert"), None),
        P(),
        P(),
        P("expert", None, None),
        P("expert", None, None),
        P(),
        P("dp", "expert", None, None),
    )
    return jax.shard_map(
        body,
        mesh=mesh,
        in_specs=placed,
        out_specs=(
            P("dp", "expert", None, None),
            P(),
            P("dp", "expert", None, None),
            P(),
            P(),
            P(),
            P(("dp", "expert"), None, None),
            P(("dp", "expert"), None),
            P(),
            P(),
            P("expert", "dp", None),
            P("expert", "dp", None),
        ),
        check_vma=False,
    )
```

```python
import functools
import math

import jax
import jax.numpy as jnp
from jax import lax
from jax.experimental import pallas as pl
from jax.experimental.pallas import tpu as pltpu
from jax.sharding import PartitionSpec as P

HEADS = 16
HD = 128
FF = 1024
TOPK = 8


NORM_EPS = 1e-05
PRECISE = lax.Precision.HIGHEST


def norm_rows(values, scale_gain):
    return (
        values
        * lax.rsqrt(jnp.mean(values * values, axis=-1, keepdims=True) + NORM_EPS)
        * scale_gain
    )


VMEM_BYTES = 56 * 1024 * 1024
TILE = 256
WIDE = 512


def params():
    return pltpu.CompilerParams(vmem_limit_bytes=VMEM_BYTES)


def dot_nn(left, right):
    return jnp.dot(left, right, preferred_element_type=jnp.float32)


def dot_nt(left, right):
    return lax.dot_general(
        left, right, (((1,), (1,)), ((), ())), preferred_element_type=jnp.float32
    )


def dot_tn(left, right):
    return lax.dot_general(
        left, right, (((0,), (0,)), ((), ())), preferred_element_type=jnp.float32
    )


def turn(values, cosine, sine):
    return values * cosine + pltpu.roll(values, HD // 2, 1) * sine


def turn_back(values, cosine, sine):
    return values * cosine + pltpu.roll(values * sine, HD // 2, 1)


def head_norm(proj):
    return lax.rsqrt(jnp.mean(proj * proj, axis=-1, keepdims=True) + NORM_EPS)


def load_heads(proj_ref, cos_ref, sin_ref, gain_ref):
    rows = cos_ref.shape[0]
    proj = proj_ref[...].reshape(rows, 3 * HD)
    cosine, sine = cos_ref[...], sin_ref[...]
    q_proj, k_proj, v_proj = proj[:, :HD], proj[:, HD : 2 * HD], proj[:, 2 * HD :]
    queries = turn(q_proj * head_norm(q_proj) * gain_ref[0:1], cosine, sine).astype(jnp.bfloat16)
    keys = turn(k_proj * head_norm(k_proj) * gain_ref[1:2], cosine, sine).astype(jnp.bfloat16)
    return q_proj, k_proj, queries, keys, v_proj.astype(jnp.bfloat16)


def row_probs(queries, keys, live):
    scores = jnp.where(live, dot_nt(queries, keys), -1e30)
    expo = jnp.exp((scores - jnp.max(scores, axis=-1, keepdims=True)) * (1.0 / math.sqrt(HD)))
    return expo * (1.0 / jnp.sum(expo, axis=-1, keepdims=True))


def attend_kernel(
    owner_ref, proj_ref, cos_ref, sin_ref, live_ref, gain_ref, out_ref, q_scr, o_scr
):
    rows, slots = cos_ref.shape[0], proj_ref.shape[2]
    step = min(TILE, rows)
    _, _, queries, keys, values = load_heads(proj_ref, cos_ref, sin_ref, gain_ref)
    q_scr[...] = queries
    live = live_ref[0] > 0.0

    def chunk(i, carry):
        part = pl.ds(pl.multiple_of(i * step, step), step)
        probs = row_probs(q_scr[part, :], keys, live).astype(jnp.bfloat16)
        o_scr[part, :] = dot_nn(probs, values).astype(jnp.bfloat16)
        return carry

    lax.fori_loop(0, rows // step, chunk, 0, unroll=True)
    for r in range(proj_ref.shape[0]):
        out_ref[owner_ref[r], 0] = o_scr[r * slots : (r + 1) * slots, :]


def attend(owners, proj, cosine, sine, live, gains):
    blocks, seqs, slots, width = proj.shape
    heads, rows = width // (3 * HD), blocks * slots
    return pl.pallas_call(
        attend_kernel,
        grid_spec=pltpu.PrefetchScalarGridSpec(
            num_scalar_prefetch=1,
            grid=(seqs, heads),
            in_specs=[
                pl.BlockSpec((blocks, 1, slots, 3 * HD), lambda s, h, o: (0, s, 0, h)),
                pl.BlockSpec((rows, HD), lambda s, h, o: (0, 0)),
                pl.BlockSpec((rows, HD), lambda s, h, o: (0, 0)),
                pl.BlockSpec((1, 1, rows), lambda s, h, o: (s, 0, 0)),
                pl.BlockSpec((2, HD), lambda s, h, o: (0, 0)),
            ],
            out_specs=pl.BlockSpec((blocks, 1, slots, HD), lambda s, h, o: (0, s, 0, h)),
            scratch_shapes=[pltpu.VMEM((rows, HD), jnp.bfloat16)] * 2,
        ),
        out_shape=jax.ShapeDtypeStruct((blocks, seqs, slots, heads * HD), jnp.bfloat16),
        compiler_params=params(),
        cost_estimate=pl.CostEstimate(
            flops=4 * seqs * heads * rows * rows * HD,
            bytes_accessed=seqs * rows * width * 5,
            transcendentals=seqs * heads * rows * rows,
        ),
        name="attend",
    )(owners, proj, cosine, sine, live, gains)


def attend_back_kernel(
    owner_ref, proj_ref, grad_ref, cos_ref, sin_ref, live_ref, gain_ref, out_ref, gain_out, q_scr, dq, dk, dv
):
    rows, slots = cos_ref.shape[0], proj_ref.shape[2]
    step = min(TILE, rows)
    scale = 1.0 / math.sqrt(HD)
    q_proj, k_proj, queries, keys, values = load_heads(proj_ref, cos_ref, sin_ref, gain_ref)
    q_scr[0] = queries
    for r in range(proj_ref.shape[0]):
        q_scr[1, r * slots : (r + 1) * slots, :] = grad_ref[owner_ref[r], 0]
    dk[...] = jnp.zeros_like(dk)
    dv[...] = jnp.zeros_like(dv)
    live = live_ref[0] > 0.0

    def chunk(i, carry):
        part = pl.ds(pl.multiple_of(i * step, step), step)
        q_part, g_part = q_scr[0, part, :], q_scr[1, part, :]
        probs = row_probs(q_part, keys, live)
        prob_grad = dot_nt(g_part, values)
        row_dot = jnp.sum(probs * prob_grad, axis=-1, keepdims=True)
        score_grad = (probs * (prob_grad - row_dot)).astype(jnp.bfloat16)
        dq[part, :] = dot_nn(score_grad, keys)
        dk[...] += dot_tn(score_grad, q_part)
        dv[...] += dot_tn(probs.astype(jnp.bfloat16), g_part)
        return carry

    lax.fori_loop(0, rows // step, chunk, 0, unroll=True)
    cosine, sine = cos_ref[...], sin_ref[...]
    parts = []
    for i, (proj, grad) in enumerate(((q_proj, dq), (k_proj, dk))):
        gain, inverse = gain_ref[i : i + 1], head_norm(proj)
        back = turn_back(grad[...] * scale, cosine, sine)
        scaled = proj * inverse
        gain_out[0, 0, i : i + 1, :] = jnp.sum(back * scaled, axis=0, keepdims=True)
        back = back * gain
        parts.append(
            inverse * (back - scaled * jnp.mean(scaled * back, axis=-1, keepdims=True))
        )
    grads = jnp.concatenate(parts + [dv[...]], axis=1).astype(jnp.bfloat16)
    out_ref[...] = grads.reshape(out_ref.shape)


def attend_back(owners, proj, grads, cosine, sine, live, gains):
    blocks, seqs, slots, width = proj.shape
    heads, rows = width // (3 * HD), blocks * slots
    return pl.pallas_call(
        attend_back_kernel,
        grid_spec=pltpu.PrefetchScalarGridSpec(
            num_scalar_prefetch=1,
            grid=(seqs, heads),
            in_specs=[
                pl.BlockSpec((blocks, 1, slots, 3 * HD), lambda s, h, o: (0, s, 0, h)),
                pl.BlockSpec((blocks, 1, slots, HD), lambda s, h, o: (0, s, 0, h)),
                pl.BlockSpec((rows, HD), lambda s, h, o: (0, 0)),
                pl.BlockSpec((rows, HD), lambda s, h, o: (0, 0)),
                pl.BlockSpec((1, 1, rows), lambda s, h, o: (s, 0, 0)),
                pl.BlockSpec((2, HD), lambda s, h, o: (0, 0)),
            ],
            out_specs=[
                pl.BlockSpec((blocks, 1, slots, 3 * HD), lambda s, h, o: (0, s, 0, h)),
                pl.BlockSpec((1, 1, 2, HD), lambda s, h, o: (s, h, 0, 0)),
            ],
            scratch_shapes=[pltpu.VMEM((2, rows, HD), jnp.bfloat16)]
            + [pltpu.VMEM((rows, HD), jnp.float32)] * 3,
        ),
        out_shape=[
            jax.ShapeDtypeStruct(proj.shape, jnp.bfloat16),
            jax.ShapeDtypeStruct((seqs, heads, 2, HD), jnp.float32),
        ],
        compiler_params=params(),
        cost_estimate=pl.CostEstimate(
            flops=10 * seqs * heads * rows * rows * HD,
            bytes_accessed=seqs * rows * width * 7,
            transcendentals=seqs * heads * rows * rows,
        ),
        name="attend_back",
    )(owners, proj, grads, cosine, sine, live, gains)


def gate_column(gates_ref, index):
    gates = gates_ref[...]
    out = jnp.zeros((gates.shape[0], 1), jnp.float32)
    for e in range(gates.shape[1]):
        out = out + jnp.where(index == e, gates[:, e : e + 1], 0.0)
    return out


def fill_rows(refs, out_ref):
    base = 0
    for ref in refs:
        out_ref[base : base + ref.shape[0], :] = ref[...]
        base += ref.shape[0]


def experts_kernel(parts, held, tiles, per, count, *refs):
    x_refs, refs = refs[:parts], refs[parts:]
    hits_ref, router_ref, own_ref, gate_w, up_w, down_w = refs[:6]
    rows, gate_out, up_out, gated_out, gates_ref, mix_out, gated = refs[6 + held :]
    i = pl.program_id(0)

    @pl.when(i == 0)
    def _():
        fill_rows(x_refs, rows)
        logits = dot_nn(rows[...], router_ref[...])
        hits = hits_ref[...].astype(jnp.float32)
        lane = lax.broadcasted_iota(jnp.int32, logits.shape, 1)
        logits = jnp.where(lane < count, logits, -1e30)
        expo = jnp.exp(logits - jnp.max(logits, axis=1, keepdims=True))
        picked = jnp.where(lane < count, hits * expo / jnp.sum(expo, axis=1, keepdims=True), 0.0)
        live = jnp.sum(jnp.where(lane == count, hits, 0.0), axis=1, keepdims=True)
        gates = live * picked / jnp.sum(picked, axis=1, keepdims=True)
        for e in range(gates_ref.shape[1]):
            gates_ref[:, e : e + 1] = jnp.sum(gates * own_ref[e : e + 1], axis=1, keepdims=True)

    @pl.when(i < tiles)
    def _():
        gate = dot_nn(rows[...], gate_w[0])
        up = dot_nn(rows[...], up_w[0])
        hidden = gate / (1.0 + jnp.exp(-gate)) * up * gate_column(gates_ref, i // per)
        gate_out[...] = gate.astype(jnp.bfloat16)
        up_out[...] = up.astype(jnp.bfloat16)
        low = hidden.astype(jnp.bfloat16)
        gated_out[...] = low
        gated[:, pl.ds(pl.multiple_of(i * WIDE, WIDE), WIDE)] = low

    @pl.when(i >= tiles)
    def _():
        mix_out[...] = dot_nn(gated[...], down_w[...]).astype(jnp.bfloat16)


def experts_forward(xs, hits, router, own, count, w_in, w_down, held, base, total):
    experts, width, _ = w_in.shape
    hidden = w_down.shape[0]
    rows = sum(x.shape[0] for x in xs)
    place = base // rows
    tiles, per, outs = hidden // WIDE, FF // WIDE, width // WIDE
    clamp = lambda i: jnp.minimum(i, tiles - 1)
    later = lambda i: jnp.maximum(i - tiles, 0)
    keep = pl.BlockSpec((rows, WIDE), lambda i: (place, clamp(i)))
    known = len(xs) + 6
    lanes = router.shape[1]
    return pl.pallas_call(
        functools.partial(experts_kernel, len(xs), len(held), tiles, per, count),
        grid=(tiles + outs,),
        in_specs=[pl.BlockSpec(x.shape, lambda i: (0, 0)) for x in xs]
        + [
            pl.BlockSpec((rows, lanes), lambda i: (0, 0)),
            pl.BlockSpec((width, lanes), lambda i: (0, 0)),
            pl.BlockSpec((experts, lanes), lambda i: (0, 0)),
            pl.BlockSpec((1, width, WIDE), lambda i: (clamp(i) // per, 0, clamp(i) % per)),
            pl.BlockSpec((1, width, WIDE), lambda i: (clamp(i) // per, 0, per + clamp(i) % per)),
            pl.BlockSpec((hidden, WIDE), lambda i: (0, later(i))),
        ]
        + [pl.BlockSpec(memory_space=pl.ANY)] * len(held),
        out_specs=[pl.BlockSpec((rows, width), lambda i: (place, 0))]
        + [keep] * 3
        + [
            pl.BlockSpec((rows, experts), lambda i: (0, 0)),
            pl.BlockSpec((rows, WIDE), lambda i: (0, later(i))),
        ],
        out_shape=[jax.ShapeDtypeStruct((total, width), jnp.bfloat16)]
        + [jax.ShapeDtypeStruct((total, hidden), jnp.bfloat16)] * 3
        + [
            jax.ShapeDtypeStruct((rows, experts), jnp.float32),
            jax.ShapeDtypeStruct((rows, width), jnp.bfloat16),
        ],
        scratch_shapes=[pltpu.VMEM((rows, hidden), jnp.bfloat16)],
        input_output_aliases={known + i: i for i in range(len(held))},
        compiler_params=params(),
        cost_estimate=pl.CostEstimate(
            flops=6 * rows * hidden * width,
            bytes_accessed=6 * hidden * width + 10 * rows * width,
            transcendentals=rows * hidden,
        ),
        name="experts_forward",
    )(*xs, hits, router, own, w_in, w_in, w_down, *held)


def experts_back_kernel(parts, held, tiles, per, *refs):
    c_refs, refs = refs[:parts], refs[parts:]
    gates_ref, own_ref, gate_ref, up_ref, down_w, in_w = refs[:6]
    rows, gate_out, up_out, score_out, grad_out, gate_grads, up_grads = refs[6 + held :]
    i = pl.program_id(0)

    @pl.when(i == 0)
    def _():
        fill_rows(c_refs, rows)

    @pl.when(i < tiles)
    def _():
        raw = dot_nt(rows[...], down_w[...])
        gate, up = gate_ref[...].astype(jnp.float32), up_ref[...].astype(jnp.float32)
        sigmoid = 1.0 / (1.0 + jnp.exp(-gate))
        silu = gate * sigmoid
        score = jnp.sum(silu * up * raw, axis=1, keepdims=True)
        own = own_ref[...]
        place = sum(jnp.where(i // per == e, own[e : e + 1], 0.0) for e in range(own.shape[0]))
        mine = score * place
        score_out[...] = jnp.where(i == 0, mine, score_out[...] + mine)
        grad = raw * gate_column(gates_ref, i // per)
        gate_low = (grad * up * (sigmoid + silu * (1.0 - sigmoid))).astype(jnp.bfloat16)
        up_low = (grad * silu).astype(jnp.bfloat16)
        gate_out[...] = gate_low
        up_out[...] = up_low
        part = pl.ds(pl.multiple_of(i * WIDE, WIDE), WIDE)
        gate_grads[:, part] = gate_low
        up_grads[:, part] = up_low

    @pl.when(i >= tiles)
    def _():
        total = 0.0
        for e in range(in_w.shape[0]):
            part = slice(e * FF, (e + 1) * FF)
            total = total + dot_nt(gate_grads[:, part], in_w[e, :, :FF])
            total = total + dot_nt(up_grads[:, part], in_w[e, :, FF:])
        grad_out[...] = total.astype(jnp.bfloat16)


def experts_backward(outs, gates, own, gate, up, w_in, w_down, held, base):
    experts, width, _ = w_in.shape
    hidden, total = w_down.shape[0], gate.shape[0]
    rows = sum(o.shape[0] for o in outs)
    place = base // rows
    tiles, per, last = hidden // WIDE, FF // WIDE, width // WIDE
    clamp = lambda i: jnp.minimum(i, tiles - 1)
    later = lambda i: jnp.maximum(i - tiles, 0)
    keep = pl.BlockSpec((rows, WIDE), lambda i: (place, clamp(i)))
    known, lanes = len(outs) + 6, own.shape[1]
    return pl.pallas_call(
        functools.partial(experts_back_kernel, len(outs), len(held), tiles, per),
        grid=(tiles + last,),
        in_specs=[pl.BlockSpec(o.shape, lambda i: (0, 0)) for o in outs]
        + [
            pl.BlockSpec((rows, experts), lambda i: (0, 0)),
            pl.BlockSpec((experts, lanes), lambda i: (0, 0)),
            keep,
            keep,
            pl.BlockSpec((WIDE, width), lambda i: (clamp(i), 0)),
            pl.BlockSpec((experts, WIDE, 2 * FF), lambda i: (0, later(i), 0)),
        ]
        + [pl.BlockSpec(memory_space=pl.ANY)] * len(held),
        out_specs=[
            pl.BlockSpec((rows, width), lambda i: (place, 0)),
            keep,
            keep,
            pl.BlockSpec((rows, lanes), lambda i: (0, 0)),
            pl.BlockSpec((rows, WIDE), lambda i: (0, later(i))),
        ],
        out_shape=[jax.ShapeDtypeStruct((total, width), jnp.bfloat16)]
        + [jax.ShapeDtypeStruct((total, hidden), jnp.bfloat16)] * 2
        + [
            jax.ShapeDtypeStruct((rows, lanes), jnp.float32),
            jax.ShapeDtypeStruct((rows, width), jnp.bfloat16),
        ],
        scratch_shapes=[pltpu.VMEM((rows, hidden), jnp.bfloat16)] * 2,
        input_output_aliases={known + i: i for i in range(len(held))},
        compiler_params=params(),
        cost_estimate=pl.CostEstimate(
            flops=6 * rows * hidden * width,
            bytes_accessed=6 * hidden * width + 12 * rows * width,
            transcendentals=rows * hidden,
        ),
        name="experts_backward",
    )(*outs, gates, own, gate, up, w_down, w_in, *held)


def ring_order(size):
    return list(range(0, size, 2)) + list(range(size - 1, 0, -2))


def ring_shift(rows, order, step):
    size = len(order)
    pairs = [(order[i], order[(i + step) % size]) for i in range(size)]
    return lax.ppermute(rows, "expert", pairs)


class Gather:
    def __init__(self, rows, order, name):
        self.order, self.half, self.done, self.name = order, len(order) // 2, 0, name
        self.blocks = {0: rows}

    def step(self, *waits):
        self.done = s = self.done + 1
        ahead, back = self.blocks[1 - s], self.blocks[s - 1]
        if s == self.half:
            cut = ahead.shape[0] // 2
            ahead, back = ahead[:cut], back[cut:]
        if waits:
            ahead, back = lax.optimization_barrier((ahead, back, *waits))[:2]
        with jax.named_scope(self.name):
            ahead, back = ring_shift(ahead, self.order, 1), ring_shift(back, self.order, -1)
        if s == self.half:
            self.parts = ahead, back
        else:
            self.blocks[-s], self.blocks[s] = ahead, back


    def join(self, *waits):
        parts = lax.optimization_barrier((*self.parts, *waits))[:2] if waits else self.parts
        self.blocks[self.half] = jnp.concatenate(parts, axis=0)


class Scatter:
    def __init__(self, far, order, name, *waits):
        self.order, self.cut, self.first, self.name = order, far.shape[0] // 2, True, name
        self.send(far[: self.cut], far[self.cut :], waits)

    def send(self, ahead, back, waits):
        ahead, back = ahead.astype(jnp.bfloat16), back.astype(jnp.bfloat16)
        if waits:
            ahead, back = lax.optimization_barrier((ahead, back, *waits))[:2]
        self.sent = (ahead, back)
        with jax.named_scope(self.name):
            self.ahead = ring_shift(ahead, self.order, 1).astype(jnp.float32)
            self.back = ring_shift(back, self.order, -1).astype(jnp.float32)

    def step(self, mine, other, *waits):
        mine, other = mine.astype(jnp.float32), other.astype(jnp.float32)
        if self.first:
            cut, self.first = self.cut, False
            mine = jnp.concatenate([mine[:cut] + self.ahead, mine[cut:]], axis=0)
            other = jnp.concatenate([other[:cut], other[cut:] + self.back], axis=0)
        else:
            mine, other = mine + self.ahead, other + self.back
        self.send(mine, other, waits)

    def finish(self, own):
        return own.astype(jnp.float32) + self.ahead + self.back


def offsets_of(size):
    half = size // 2
    out = [0]
    for step in range(1, half):
        out += [-step, step]
    return out + [half]


def sum_over(values, axis):
    size, step = lax.axis_size(axis), 1
    while step < size:
        values = values + lax.ppermute(values, axis, [(i, i ^ step) for i in range(size)])
        step *= 2
    return values


class Sum:
    def __init__(self, values):
        self.values = values
        self.left = [
            (axis, 1 << b)
            for axis in ("expert", "dp")
            for b in range(lax.axis_size(axis).bit_length() - 1)
        ]

    def step(self, *waits):
        if not self.left:
            return
        axis, bit = self.left.pop(0)
        values = after(self.values, *waits) if waits else self.values
        with jax.named_scope("sum_small"):
            other = lax.ppermute(values, axis, [(i, i ^ bit) for i in range(lax.axis_size(axis))])
        self.values = values + other

    def finish(self):
        while self.left:
            self.step()
        return self.values


def after(values, *others):
    return lax.optimization_barrier((values, *others))[0]


def weight_kernel(parts, adds, outs, index_ref, *refs):
    left_refs, right_ref, refs = refs[:parts], refs[parts], refs[parts + 1 :]
    add_refs, out_refs, left = refs[:adds], refs[adds : adds + outs], refs[-1]
    tile = left_refs[0].shape[1]

    @pl.when(pl.program_id(0) == 0)
    def _():
        for p, ref in enumerate(left_refs):
            left[p * tile : (p + 1) * tile, :] = ref[...].T

    total = dot_nn(left[...], right_ref[...])
    height = parts * tile // outs
    for o, out_ref in enumerate(out_refs):
        for p in range(parts // outs):
            at = o * height + p * tile
            part = total[at : at + tile]
            if adds:
                part = part + add_refs[at // tile][...].astype(jnp.float32)
            out_ref[p * tile : (p + 1) * tile, :] = part.astype(out_ref.dtype)


def weight_part(left, right, tile, columns, add, add_rows, types, name):
    rows, width, wide = left.shape[0], right.shape[1], WIDE
    parts, adds, outs = len(columns), len(add_rows), len(types)
    places = list(columns) + list(add_rows)
    height = parts * tile // outs
    in_specs = [
        pl.BlockSpec((rows, tile), lambda j, at, p=p: (0, at[p])) for p in range(parts)
    ] + [pl.BlockSpec((rows, wide), lambda j, at: (0, j))]
    in_specs += [
        pl.BlockSpec((tile, wide), lambda j, at, p=p: (at[p], j))
        for p in range(parts, len(places))
    ]
    return pl.pallas_call(
        functools.partial(weight_kernel, parts, adds, outs),
        grid_spec=pltpu.PrefetchScalarGridSpec(
            num_scalar_prefetch=1,
            grid=(width // wide,),
            in_specs=in_specs,
            out_specs=[pl.BlockSpec((height, wide), lambda j, at: (0, j))] * outs,
            scratch_shapes=[pltpu.VMEM((parts * tile, rows), jnp.bfloat16)],
        ),
        out_shape=[jax.ShapeDtypeStruct((height, width), t) for t in types],
        compiler_params=params(),
        cost_estimate=pl.CostEstimate(
            flops=2 * rows * parts * tile * width,
            bytes_accessed=2 * rows * (parts * tile + width) + 4 * parts * tile * width,
            transcendentals=0,
        ),
        name=name,
    )(jnp.stack([jnp.asarray(p, jnp.int32) for p in places]), *[left] * parts, right, *[add] * adds)


class GroupSum:
    def __init__(self, left, right, outer, name):
        self.left, self.right, self.outer, self.name = left, right, outer, name
        self.size = lax.axis_size("dp")
        me = lax.axis_index("dp")
        self.core, self.pair = me % 2, me // 2
        self.tile = left.shape[1] // outer // self.size

    def tiles(self, core, pairs):
        return [4 * o + 2 * pair + core for pair in pairs for o in range(self.outer)]

    def first(self, *waits):
        left = after(self.left, *waits) if waits else self.left
        if self.size != 4:
            terms = dot_tn(left, self.right).astype(jnp.bfloat16)
            terms = terms.reshape(self.outer, -1, terms.shape[1])
            self.far = self.near = lax.psum_scatter(terms, "dp", scatter_dimension=1, tiled=True)
            return
        columns = self.tiles(1 - self.core, (0, 1))
        (self.far,) = weight_part(
            left, self.right, self.tile, columns, None, [], [jnp.bfloat16], self.name
        )
        with jax.named_scope(self.name + "_cores"):
            self.got = lax.ppermute(self.far, "dp", [(i, i ^ 1) for i in range(4)])

    def second(self, *waits):
        if self.size != 4:
            return
        left = after(self.left, *waits) if waits else self.left
        pairs = (1 - self.pair, self.pair)
        self.near, self.own = weight_part(
            left,
            self.right,
            self.tile,
            self.tiles(self.core, pairs),
            self.got,
            [pair * self.outer + o for pair in pairs for o in range(self.outer)],
            [jnp.bfloat16, jnp.float32],
            self.name,
        )
        with jax.named_scope(self.name + "_groups"):
            self.back = lax.ppermute(self.near, "dp", [(i, i ^ 2) for i in range(4)])

    def total(self):
        if self.size != 4:
            return self.far.reshape(-1, self.far.shape[-1]).astype(jnp.float32)
        return self.own + self.back.astype(jnp.float32)


def body(
    tokens,
    lengths,
    routes,
    attn_gain,
    q_gain,
    k_gain,
    qkv_weight,
    out_weight,
    ffn_gain,
    router_weight,
    expert_in,
    expert_out,
    balance_coef,
    cotangent,
):
    bf16, f32 = jnp.bfloat16, jnp.float32
    n_expert = lax.axis_size("expert")
    group_index = lax.axis_index("dp")
    member = lax.axis_index("expert")
    slot_count = tokens.shape[1]
    seq_count = tokens.shape[2]
    width = tokens.shape[3]
    experts_here = expert_in.shape[0]
    experts_all = experts_here * n_expert
    tok_rows = slot_count * seq_count
    full_len = slot_count * n_expert
    heads_here = HEADS // n_expert
    cols = heads_here * HD

    order = ring_order(n_expert)
    offsets = offsets_of(n_expert)
    half = n_expert // 2
    table = [[order[(order.index(m) + r) % n_expert] for r in offsets] for m in range(n_expert)]
    owners = lax.dynamic_index_in_dim(jnp.array(table, jnp.int32), member, 0, False)
    owner = {r: owners[i] for i, r in enumerate(offsets)}

    def blockwise(blocks, axis=0):
        return jnp.concatenate([blocks[r] for r in offsets], axis=axis)

    def to_rows(values):
        return jnp.swapaxes(values[0], 0, 1).reshape(tok_rows, values.shape[3])

    def from_rows(rows):
        return jnp.swapaxes(rows.reshape(seq_count, slot_count, width), 0, 1)[None]

    seq_lens = lengths[group_index]
    slot_ids = member * slot_count + jnp.arange(slot_count)
    valid_rows = (slot_ids[None, :] < seq_lens[:, None]).astype(f32).reshape(tok_rows)
    all_slots = (owners[:, None] * slot_count + jnp.arange(slot_count)[None, :]).reshape(full_len)
    key_live = (all_slots[None, :] < seq_lens[:, None]).astype(f32)[:, None, :]
    inv_freq = jnp.exp(
        jnp.arange(HD // 2, dtype=f32) * (-2.0 * math.log(10000.0) / HD)
    )
    angles = all_slots.astype(f32)[:, None] * inv_freq[None, :]
    cosine, sine = jnp.cos(angles), jnp.sin(angles)
    cosine = jnp.concatenate([cosine, cosine], axis=1)
    sine = jnp.concatenate([-sine, sine], axis=1)
    head_gains = jnp.stack([q_gain, k_gain])

    inputs = to_rows(tokens).astype(f32)
    normed = norm_rows(inputs, attn_gain)

    lanes = 128
    picked_ids = to_rows(routes)
    chosen = jnp.sum(
        (picked_ids[:, :, None] == jnp.arange(experts_all)[None, None, :]).astype(f32), axis=1
    )
    hits = jnp.concatenate([chosen, valid_rows[:, None]], axis=1)
    hits = jnp.pad(hits, ((0, 0), (0, lanes - experts_all - 1)))
    normed_ring = Gather(
        jnp.concatenate([normed.astype(bf16), hits.astype(bf16)], axis=1), order, "ring_normed"
    )
    normed_ring.step()

    row_count = qkv_weight.shape[0]
    w_cols = qkv_weight.reshape(row_count, 3, n_expert, heads_here, HD).transpose(2, 0, 3, 1, 4)
    w_cols = lax.all_to_all(
        after(
            w_cols.reshape(n_expert, row_count, 3 * cols),
            normed_ring.blocks[1],
            normed_ring.blocks[-1],
        ),
        "expert",
        split_axis=0,
        concat_axis=0,
        tiled=True,
    )
    w_qkv = lax.all_gather(w_cols.reshape(-1, 3 * cols), "dp", axis=0, tiled=True)
    router_pad = jnp.pad(router_weight, ((0, 0), (0, lanes - experts_all)))
    own_ids = member * experts_here + jnp.arange(experts_here)
    own_rows = (own_ids[:, None] == jnp.arange(lanes)[None, :]).astype(f32)

    for _ in range(half - 2):
        normed_ring.step()
    w_out = lax.all_gather(
        after(out_weight, normed_ring.blocks[half - 1], normed_ring.blocks[1 - half]),
        "expert",
        axis=0,
        tiled=True,
    )
    normed_ring.step()
    normed_ring.join()
    hits_of = {r: normed_ring.blocks[r][:, width:] for r in offsets}
    normed_all = blockwise({r: normed_ring.blocks[r][:, :width] for r in offsets})
    hits_all = blockwise(hits_of).astype(f32)
    counts = jnp.sum(hits_all[:, experts_all : experts_all + 1] * hits_all, axis=0)
    count_total = sum_over(counts[:experts_all], "dp")
    n_valid = jnp.sum(lengths).astype(f32)
    fraction = count_total / (TOPK * n_valid)
    cot_rows = to_rows(cotangent)
    cot_ring = Gather(cot_rows, order, "ring_cotangent")
    cot_ring.step(normed_all)

    project = dot_nn(normed_all, w_qkv).reshape(n_expert, seq_count, slot_count, 3 * cols)
    attended = attend(owners, project, cosine, sine, key_live, head_gains)
    w_out = lax.all_gather(after(w_out, attended), "dp", axis=0, tiled=True)
    attended = after(attended, cot_ring.blocks[1], cot_ring.blocks[-1])
    cot_ring.step(attended)
    attended_low = lax.all_to_all(
        attended.reshape(n_expert, tok_rows, cols), "expert", split_axis=0, concat_axis=0, tiled=True
    )
    attended_low = jnp.swapaxes(attended_low, 0, 1).reshape(tok_rows, width)
    residual = inputs + dot_nn(attended_low, w_out)
    ffn_normed, ffn_back = jax.vjp(norm_rows, residual, ffn_gain)
    ffn_low = ffn_normed.astype(bf16)
    for _ in range(half - 3):
        cot_ring.step(residual)
    ffn_ring = Gather(ffn_low, order, "ring_ffn")
    ffn_ring.step()

    live = valid_rows[:, None]
    router_probs = jax.nn.softmax(dot_nn(ffn_low, router_weight), axis=-1)
    picked = chosen * router_probs
    picked_total = jnp.sum(picked, axis=-1, keepdims=True)
    prob_sums = jnp.sum(live * router_probs, axis=0)
    groups = [[0]] + [[-s, s] for s in range(1, half)] + [[half]]
    bases = [(n_expert - 2) * tok_rows]
    bases += [2 * s * tok_rows for s in range(half - 1)] + [(n_expert - 1) * tok_rows]
    w_down = expert_out.reshape(experts_here * FF, width)
    all_rows = n_expert * tok_rows

    def split(rows, group):
        return {r: rows[i * tok_rows : (i + 1) * tok_rows] for i, r in enumerate(group)}

    held, mix_blocks, group_gates = [], {}, []
    for i, g in enumerate(groups):
        *held, gates, mixed = experts_forward(
            [
                after(ffn_ring.blocks[r], cot_ring.blocks[half - 1], cot_ring.blocks[1 - half])
                if i == 2
                else ffn_ring.blocks[r]
                for r in g
            ],
            jnp.concatenate([hits_of[r] for r in g], axis=0),
            router_pad,
            own_rows,
            experts_all,
            expert_in,
            w_down,
            held,
            bases[i],
            all_rows,
        )
        group_gates.append(gates)
        mix_blocks.update(split(mixed, g))
        if i < half - 1:
            ffn_ring.step(mixed)
        if i == half - 1:
            ffn_ring.join()
        if i == 1:
            cot_ring.step(mixed)
    cot_ring.join(gates)
    x_all, gate_all, up_all, gated_all = held
    held, ffn_sum = [], None
    mix_sum = Scatter(mix_blocks[half], order, "ring_mixture")
    ready = ()
    for i in reversed(range(len(groups))):
        g = groups[i]
        *held, scores, grads = experts_backward(
            [cot_ring.blocks[r] for r in g],
            after(group_gates[i], *ready) if ready else group_gates[i],
            own_rows,
            gate_all,
            up_all,
            expert_in,
            w_down,
            held,
            bases[i],
        )
        grads = jnp.concatenate([grads, scores.astype(bf16)], axis=1)
        if i == half:
            ffn_sum = Scatter(grads, order, "ring_ffn_grad")
        elif i > 0:
            ffn_sum.step(grads[tok_rows:], grads[:tok_rows])
        if 1 < i < half:
            mix_sum.step(mix_blocks[i], mix_blocks[-i], grads)
        ready = (*mix_sum.sent, *ffn_sum.sent)
    out_all, gate_grad_all, up_grad_all = held
    sums = [
        GroupSum(gated_all, out_all, experts_here, "weights_out"),
        GroupSum(x_all, gate_grad_all, 1, "weights_gate"),
        GroupSum(x_all, up_grad_all, 1, "weights_up"),
    ]
    sums[0].first()
    ffn_grad = ffn_sum.finish(after(grads, sums[0].far))
    gate_grads = ffn_grad[:, width : width + experts_all] * chosen
    ffn_grad = ffn_grad[:, :width]
    mix_sum.step(mix_blocks[1], mix_blocks[-1], ffn_grad)
    picked_grad = (
        live
        * chosen
        * (
            gate_grads / picked_total
            - jnp.sum(gate_grads * picked, axis=-1, keepdims=True) / (picked_total * picked_total)
        )
    )
    prob_grad = picked_grad + balance_coef * experts_all * fraction[None, :] / n_valid * live
    logit_grad = router_probs * (
        prob_grad - jnp.sum(router_probs * prob_grad, axis=-1, keepdims=True)
    )
    ffn_grad = ffn_grad + jnp.dot(logit_grad, router_weight.astype(f32).T, precision=PRECISE)
    router_terms = jnp.dot(ffn_low.astype(f32).T, logit_grad, precision=PRECISE)
    residual_norm_grad, ffn_gain_terms = ffn_back(ffn_grad)
    residual_grad = cot_rows.astype(f32) * live + residual_norm_grad
    branch_grad = residual_grad.astype(bf16)

    attended_grad = dot_nt(branch_grad, w_out).astype(bf16)
    attended_grad = lax.all_to_all(
        jnp.swapaxes(attended_grad.reshape(tok_rows, n_expert, cols), 0, 1),
        "expert",
        split_axis=0,
        concat_axis=0,
        tiled=True,
    ).reshape(attended.shape)

    output_terms = dot_tn(attended_low, branch_grad).astype(bf16)
    out_share = lax.psum_scatter(output_terms, "dp", scatter_dimension=0, tiled=True)
    sums[0].second(branch_grad)
    attended_grad = after(attended_grad, sums[0].near, output_terms)

    block_rows = residual + mix_sum.finish(mix_blocks[0])
    attended_grad = after(attended_grad, block_rows)
    proj_grad, gain_parts = attend_back(
        owners, project, attended_grad, cosine, sine, key_live, head_gains
    )
    proj_grad = proj_grad.reshape(all_rows, 3 * cols)
    normed_terms = dot_nt(proj_grad, w_qkv).astype(bf16)
    normed_parts = {
        r: normed_terms[i * tok_rows : (i + 1) * tok_rows] for i, r in enumerate(offsets)
    }
    normed_sum = Scatter(normed_parts[half], order, "ring_normed_grad")
    attn_gain_terms = (
        jnp.sum(normed_terms.astype(f32) * normed_all.astype(f32), axis=0) / attn_gain
    )
    head_gain_grads = jnp.sum(gain_parts, axis=(0, 1)).reshape(-1)
    small = Sum(
        jnp.concatenate(
            [
                router_terms.reshape(-1),
                ffn_gain_terms,
                attn_gain_terms,
                head_gain_grads,
                prob_sums,
            ]
        )
    )
    sums[1].first(normed_terms)
    waits = [sums[1].far]
    for s in range(half - 1, 0, -1):
        normed_sum.step(normed_parts[s], normed_parts[-s], *waits)
        waits = []
        if s == half - 1:
            sums[1].second(normed_terms)
            proj_terms = dot_tn(after(normed_all, sums[1].near), proj_grad).astype(bf16)
            waits = [sums[1].near, proj_terms]
        if s == half - 2:
            sums[2].first(proj_terms)
            waits = [sums[2].far]
        if s == half - 3:
            sums[2].second(proj_terms)
    proj_share = lax.psum_scatter(proj_terms, "dp", scatter_dimension=0, tiled=True)
    normed_grad = normed_sum.finish(after(normed_parts[0], sums[2].near))
    grad_out = lax.psum_scatter(
        out_share, "expert", scatter_dimension=0, tiled=True
    ).astype(f32)
    (input_norm_grad,) = jax.vjp(lambda v: norm_rows(v, attn_gain), inputs)[1](normed_grad)
    grad_tokens = from_rows(residual_grad + input_norm_grad)
    block_out = from_rows(block_rows)
    grad_expert_out = sums[0].total().reshape(experts_here, -1, width)
    shares = [sums[1].total(), sums[2].total()]
    grad_expert_in = jnp.stack(
        [
            jnp.concatenate([s[:, e * FF : (e + 1) * FF] for s in shares], axis=1)
            for e in range(experts_here)
        ]
    )

    grad_qkv = lax.all_to_all(
        proj_share.reshape(n_expert, row_count, 3 * cols),
        "expert",
        split_axis=0,
        concat_axis=0,
        tiled=True,
    ).reshape(n_expert, row_count, heads_here, 3, HD)
    grad_qkv = grad_qkv.transpose(1, 3, 0, 2, 4).reshape(row_count, 3, width).astype(f32)

    small.step(normed_grad)
    for _ in range(n_expert.bit_length() - 2):
        small.step()
    small.step(grad_qkv)
    small = small.finish()
    places, pieces = 0, []
    for size in (width * experts_all, width, width, HD, HD, experts_all):
        pieces.append(small[places : places + size])
        places += size
    grad_router, grad_ffn_gain, grad_attn_gain, grad_q_gain, grad_k_gain, prob_total = pieces
    balance_loss = balance_coef * experts_all * jnp.sum(fraction * (prob_total / n_valid))
    return (
        block_out,
        balance_loss,
        grad_tokens,
        grad_attn_gain,
        grad_q_gain,
        grad_k_gain,
        grad_qkv,
        grad_out,
        grad_ffn_gain,
        grad_router.reshape(width, experts_all),
        grad_expert_in,
        grad_expert_out,
    )


def solution(mesh):
    placed = (
        P("dp", "expert", None, None),
        P(),
        P("dp", "expert", None, None),
        P(),
        P(),
        P(),
        P(("dp", "expert"), None, None),
        P(("dp", "expert"), None),
        P(),
        P(),
        P("expert", None, None),
        P("expert", None, None),
        P(),
        P("dp", "expert", None, None),
    )
    return jax.shard_map(
        body,
        mesh=mesh,
        in_specs=placed,
        out_specs=(
            P("dp", "expert", None, None),
            P(),
            P("dp", "expert", None, None),
            P(),
            P(),
            P(),
            P(("dp", "expert"), None, None),
            P(("dp", "expert"), None),
            P(),
            P(),
            P("expert", "dp", None),
            P("expert", "dp", None),
        ),
        check_vma=False,
    )
```

```python
import functools
import math

import jax
import jax.numpy as jnp
from jax import lax
from jax.experimental import pallas as pl
from jax.experimental.pallas import tpu as pltpu
from jax.sharding import PartitionSpec as P

HEADS = 16
HD = 128
FF = 1024
TOPK = 8


NORM_EPS = 1e-05
PRECISE = lax.Precision.HIGHEST


def norm_rows(values, scale_gain):
    return (
        values
        * lax.rsqrt(jnp.mean(values * values, axis=-1, keepdims=True) + NORM_EPS)
        * scale_gain
    )


VMEM_BYTES = 56 * 1024 * 1024
TILE = 256
WIDE = 512


def params():
    return pltpu.CompilerParams(vmem_limit_bytes=VMEM_BYTES)


def dot_nn(left, right):
    return jnp.dot(left, right, preferred_element_type=jnp.float32)


def dot_nt(left, right):
    return lax.dot_general(
        left, right, (((1,), (1,)), ((), ())), preferred_element_type=jnp.float32
    )


def dot_tn(left, right):
    return lax.dot_general(
        left, right, (((0,), (0,)), ((), ())), preferred_element_type=jnp.float32
    )


def turn(values, cosine, sine):
    return values * cosine + pltpu.roll(values, HD // 2, 1) * sine


def turn_back(values, cosine, sine):
    return values * cosine + pltpu.roll(values * sine, HD // 2, 1)


def head_norm(proj):
    return lax.rsqrt(jnp.mean(proj * proj, axis=-1, keepdims=True) + NORM_EPS)


def load_heads(proj_ref, cos_ref, sin_ref, gain_ref):
    rows = cos_ref.shape[0]
    proj = proj_ref[...].reshape(rows, 3 * HD)
    cosine, sine = cos_ref[...], sin_ref[...]
    q_proj, k_proj, v_proj = proj[:, :HD], proj[:, HD : 2 * HD], proj[:, 2 * HD :]
    queries = turn(q_proj * head_norm(q_proj) * gain_ref[0:1], cosine, sine).astype(jnp.bfloat16)
    keys = turn(k_proj * head_norm(k_proj) * gain_ref[1:2], cosine, sine).astype(jnp.bfloat16)
    return q_proj, k_proj, queries, keys, v_proj.astype(jnp.bfloat16)


def row_probs(queries, keys, live):
    scores = jnp.where(live, dot_nt(queries, keys), -1e30)
    expo = jnp.exp((scores - jnp.max(scores, axis=-1, keepdims=True)) * (1.0 / math.sqrt(HD)))
    return expo * (1.0 / jnp.sum(expo, axis=-1, keepdims=True))


def attend_kernel(
    owner_ref, proj_ref, cos_ref, sin_ref, live_ref, gain_ref, out_ref, q_scr, o_scr
):
    rows, slots = cos_ref.shape[0], proj_ref.shape[2]
    step = min(TILE, rows)
    _, _, queries, keys, values = load_heads(proj_ref, cos_ref, sin_ref, gain_ref)
    q_scr[...] = queries
    live = live_ref[0] > 0.0

    def chunk(i, carry):
        part = pl.ds(pl.multiple_of(i * step, step), step)
        probs = row_probs(q_scr[part, :], keys, live).astype(jnp.bfloat16)
        o_scr[part, :] = dot_nn(probs, values).astype(jnp.bfloat16)
        return carry

    lax.fori_loop(0, rows // step, chunk, 0, unroll=True)
    for r in range(proj_ref.shape[0]):
        out_ref[owner_ref[r], 0] = o_scr[r * slots : (r + 1) * slots, :]


def attend(owners, proj, cosine, sine, live, gains):
    blocks, seqs, slots, width = proj.shape
    heads, rows = width // (3 * HD), blocks * slots
    return pl.pallas_call(
        attend_kernel,
        grid_spec=pltpu.PrefetchScalarGridSpec(
            num_scalar_prefetch=1,
            grid=(seqs, heads),
            in_specs=[
                pl.BlockSpec((blocks, 1, slots, 3 * HD), lambda s, h, o: (0, s, 0, h)),
                pl.BlockSpec((rows, HD), lambda s, h, o: (0, 0)),
                pl.BlockSpec((rows, HD), lambda s, h, o: (0, 0)),
                pl.BlockSpec((1, 1, rows), lambda s, h, o: (s, 0, 0)),
                pl.BlockSpec((2, HD), lambda s, h, o: (0, 0)),
            ],
            out_specs=pl.BlockSpec((blocks, 1, slots, HD), lambda s, h, o: (0, s, 0, h)),
            scratch_shapes=[pltpu.VMEM((rows, HD), jnp.bfloat16)] * 2,
        ),
        out_shape=jax.ShapeDtypeStruct((blocks, seqs, slots, heads * HD), jnp.bfloat16),
        compiler_params=params(),
        cost_estimate=pl.CostEstimate(
            flops=4 * seqs * heads * rows * rows * HD,
            bytes_accessed=seqs * rows * width * 5,
            transcendentals=seqs * heads * rows * rows,
        ),
        name="attend",
    )(owners, proj, cosine, sine, live, gains)


def attend_back_kernel(
    owner_ref, proj_ref, grad_ref, cos_ref, sin_ref, live_ref, gain_ref, out_ref, gain_out, q_scr, dq, dk, dv
):
    rows, slots = cos_ref.shape[0], proj_ref.shape[2]
    step = min(TILE, rows)
    scale = 1.0 / math.sqrt(HD)
    q_proj, k_proj, queries, keys, values = load_heads(proj_ref, cos_ref, sin_ref, gain_ref)
    q_scr[0] = queries
    for r in range(proj_ref.shape[0]):
        q_scr[1, r * slots : (r + 1) * slots, :] = grad_ref[owner_ref[r], 0]
    dk[...] = jnp.zeros_like(dk)
    dv[...] = jnp.zeros_like(dv)
    live = live_ref[0] > 0.0

    def chunk(i, carry):
        part = pl.ds(pl.multiple_of(i * step, step), step)
        q_part, g_part = q_scr[0, part, :], q_scr[1, part, :]
        probs = row_probs(q_part, keys, live)
        prob_grad = dot_nt(g_part, values)
        row_dot = jnp.sum(probs * prob_grad, axis=-1, keepdims=True)
        score_grad = (probs * (prob_grad - row_dot)).astype(jnp.bfloat16)
        dq[part, :] = dot_nn(score_grad, keys)
        dk[...] += dot_tn(score_grad, q_part)
        dv[...] += dot_tn(probs.astype(jnp.bfloat16), g_part)
        return carry

    lax.fori_loop(0, rows // step, chunk, 0, unroll=True)
    cosine, sine = cos_ref[...], sin_ref[...]
    parts = []
    for i, (proj, grad) in enumerate(((q_proj, dq), (k_proj, dk))):
        gain, inverse = gain_ref[i : i + 1], head_norm(proj)
        back = turn_back(grad[...] * scale, cosine, sine)
        scaled = proj * inverse
        gain_out[0, 0, i : i + 1, :] = jnp.sum(back * scaled, axis=0, keepdims=True)
        back = back * gain
        parts.append(
            inverse * (back - scaled * jnp.mean(scaled * back, axis=-1, keepdims=True))
        )
    grads = jnp.concatenate(parts + [dv[...]], axis=1).astype(jnp.bfloat16)
    out_ref[...] = grads.reshape(out_ref.shape)


def attend_back(owners, proj, grads, cosine, sine, live, gains):
    blocks, seqs, slots, width = proj.shape
    heads, rows = width // (3 * HD), blocks * slots
    return pl.pallas_call(
        attend_back_kernel,
        grid_spec=pltpu.PrefetchScalarGridSpec(
            num_scalar_prefetch=1,
            grid=(seqs, heads),
            in_specs=[
                pl.BlockSpec((blocks, 1, slots, 3 * HD), lambda s, h, o: (0, s, 0, h)),
                pl.BlockSpec((blocks, 1, slots, HD), lambda s, h, o: (0, s, 0, h)),
                pl.BlockSpec((rows, HD), lambda s, h, o: (0, 0)),
                pl.BlockSpec((rows, HD), lambda s, h, o: (0, 0)),
                pl.BlockSpec((1, 1, rows), lambda s, h, o: (s, 0, 0)),
                pl.BlockSpec((2, HD), lambda s, h, o: (0, 0)),
            ],
            out_specs=[
                pl.BlockSpec((blocks, 1, slots, 3 * HD), lambda s, h, o: (0, s, 0, h)),
                pl.BlockSpec((1, 1, 2, HD), lambda s, h, o: (s, h, 0, 0)),
            ],
            scratch_shapes=[pltpu.VMEM((2, rows, HD), jnp.bfloat16)]
            + [pltpu.VMEM((rows, HD), jnp.float32)] * 3,
        ),
        out_shape=[
            jax.ShapeDtypeStruct(proj.shape, jnp.bfloat16),
            jax.ShapeDtypeStruct((seqs, heads, 2, HD), jnp.float32),
        ],
        compiler_params=params(),
        cost_estimate=pl.CostEstimate(
            flops=10 * seqs * heads * rows * rows * HD,
            bytes_accessed=seqs * rows * width * 7,
            transcendentals=seqs * heads * rows * rows,
        ),
        name="attend_back",
    )(owners, proj, grads, cosine, sine, live, gains)


def gate_column(gates_ref, index):
    gates = gates_ref[...]
    out = jnp.zeros((gates.shape[0], 1), jnp.float32)
    for e in range(gates.shape[1]):
        out = out + jnp.where(index == e, gates[:, e : e + 1], 0.0)
    return out


def fill_rows(refs, out_ref):
    base = 0
    for ref in refs:
        out_ref[base : base + ref.shape[0], :] = ref[...]
        base += ref.shape[0]


def experts_kernel(parts, held, tiles, per, count, *refs):
    x_refs, refs = refs[:parts], refs[parts:]
    hits_ref, router_ref, own_ref, gate_w, up_w, down_w = refs[:6]
    rows, gate_out, up_out, gated_out, gates_ref, mix_out, gated = refs[6 + held :]
    i = pl.program_id(0)

    @pl.when(i == 0)
    def _():
        fill_rows(x_refs, rows)
        logits = dot_nn(rows[...], router_ref[...])
        hits = hits_ref[...].astype(jnp.float32)
        lane = lax.broadcasted_iota(jnp.int32, logits.shape, 1)
        logits = jnp.where(lane < count, logits, -1e30)
        expo = jnp.exp(logits - jnp.max(logits, axis=1, keepdims=True))
        picked = jnp.where(lane < count, hits * expo / jnp.sum(expo, axis=1, keepdims=True), 0.0)
        live = jnp.sum(jnp.where(lane == count, hits, 0.0), axis=1, keepdims=True)
        gates = live * picked / jnp.sum(picked, axis=1, keepdims=True)
        for e in range(gates_ref.shape[1]):
            gates_ref[:, e : e + 1] = jnp.sum(gates * own_ref[e : e + 1], axis=1, keepdims=True)

    @pl.when(i < tiles)
    def _():
        gate = dot_nn(rows[...], gate_w[0])
        up = dot_nn(rows[...], up_w[0])
        hidden = gate / (1.0 + jnp.exp(-gate)) * up * gate_column(gates_ref, i // per)
        gate_out[...] = gate.astype(jnp.bfloat16)
        up_out[...] = up.astype(jnp.bfloat16)
        low = hidden.astype(jnp.bfloat16)
        gated_out[...] = low
        gated[:, pl.ds(pl.multiple_of(i * WIDE, WIDE), WIDE)] = low

    @pl.when(i >= tiles)
    def _():
        mix_out[...] = dot_nn(gated[...], down_w[...]).astype(jnp.bfloat16)


def experts_forward(xs, hits, router, own, count, w_in, w_down, held, base, total):
    experts, width, _ = w_in.shape
    hidden = w_down.shape[0]
    rows = sum(x.shape[0] for x in xs)
    place = base // rows
    tiles, per, outs = hidden // WIDE, FF // WIDE, width // WIDE
    clamp = lambda i: jnp.minimum(i, tiles - 1)
    later = lambda i: jnp.maximum(i - tiles, 0)
    keep = pl.BlockSpec((rows, WIDE), lambda i: (place, clamp(i)))
    known = len(xs) + 6
    lanes = router.shape[1]
    return pl.pallas_call(
        functools.partial(experts_kernel, len(xs), len(held), tiles, per, count),
        grid=(tiles + outs,),
        in_specs=[pl.BlockSpec(x.shape, lambda i: (0, 0)) for x in xs]
        + [
            pl.BlockSpec((rows, lanes), lambda i: (0, 0)),
            pl.BlockSpec((width, lanes), lambda i: (0, 0)),
            pl.BlockSpec((experts, lanes), lambda i: (0, 0)),
            pl.BlockSpec((1, width, WIDE), lambda i: (clamp(i) // per, 0, clamp(i) % per)),
            pl.BlockSpec((1, width, WIDE), lambda i: (clamp(i) // per, 0, per + clamp(i) % per)),
            pl.BlockSpec((hidden, WIDE), lambda i: (0, later(i))),
        ]
        + [pl.BlockSpec(memory_space=pl.ANY)] * len(held),
        out_specs=[pl.BlockSpec((rows, width), lambda i: (place, 0))]
        + [keep] * 3
        + [
            pl.BlockSpec((rows, experts), lambda i: (0, 0)),
            pl.BlockSpec((rows, WIDE), lambda i: (0, later(i))),
        ],
        out_shape=[jax.ShapeDtypeStruct((total, width), jnp.bfloat16)]
        + [jax.ShapeDtypeStruct((total, hidden), jnp.bfloat16)] * 3
        + [
            jax.ShapeDtypeStruct((rows, experts), jnp.float32),
            jax.ShapeDtypeStruct((rows, width), jnp.bfloat16),
        ],
        scratch_shapes=[pltpu.VMEM((rows, hidden), jnp.bfloat16)],
        input_output_aliases={known + i: i for i in range(len(held))},
        compiler_params=params(),
        cost_estimate=pl.CostEstimate(
            flops=6 * rows * hidden * width,
            bytes_accessed=6 * hidden * width + 10 * rows * width,
            transcendentals=rows * hidden,
        ),
        name="experts_forward",
    )(*xs, hits, router, own, w_in, w_in, w_down, *held)


def experts_back_kernel(parts, held, tiles, per, *refs):
    c_refs, refs = refs[:parts], refs[parts:]
    gates_ref, own_ref, gate_ref, up_ref, down_w, in_w = refs[:6]
    rows, gate_out, up_out, score_out, grad_out, gate_grads, up_grads = refs[6 + held :]
    i = pl.program_id(0)

    @pl.when(i == 0)
    def _():
        fill_rows(c_refs, rows)

    @pl.when(i < tiles)
    def _():
        raw = dot_nt(rows[...], down_w[...])
        gate, up = gate_ref[...].astype(jnp.float32), up_ref[...].astype(jnp.float32)
        sigmoid = 1.0 / (1.0 + jnp.exp(-gate))
        silu = gate * sigmoid
        score = jnp.sum(silu * up * raw, axis=1, keepdims=True)
        own = own_ref[...]
        place = sum(jnp.where(i // per == e, own[e : e + 1], 0.0) for e in range(own.shape[0]))
        mine = score * place
        score_out[...] = jnp.where(i == 0, mine, score_out[...] + mine)
        grad = raw * gate_column(gates_ref, i // per)
        gate_low = (grad * up * (sigmoid + silu * (1.0 - sigmoid))).astype(jnp.bfloat16)
        up_low = (grad * silu).astype(jnp.bfloat16)
        gate_out[...] = gate_low
        up_out[...] = up_low
        part = pl.ds(pl.multiple_of(i * WIDE, WIDE), WIDE)
        gate_grads[:, part] = gate_low
        up_grads[:, part] = up_low

    @pl.when(i >= tiles)
    def _():
        total = 0.0
        for e in range(in_w.shape[0]):
            part = slice(e * FF, (e + 1) * FF)
            total = total + dot_nt(gate_grads[:, part], in_w[e, :, :FF])
            total = total + dot_nt(up_grads[:, part], in_w[e, :, FF:])
        grad_out[...] = total.astype(jnp.bfloat16)


def experts_backward(outs, gates, own, gate, up, w_in, w_down, held, base):
    experts, width, _ = w_in.shape
    hidden, total = w_down.shape[0], gate.shape[0]
    rows = sum(o.shape[0] for o in outs)
    place = base // rows
    tiles, per, last = hidden // WIDE, FF // WIDE, width // WIDE
    clamp = lambda i: jnp.minimum(i, tiles - 1)
    later = lambda i: jnp.maximum(i - tiles, 0)
    keep = pl.BlockSpec((rows, WIDE), lambda i: (place, clamp(i)))
    known, lanes = len(outs) + 6, own.shape[1]
    return pl.pallas_call(
        functools.partial(experts_back_kernel, len(outs), len(held), tiles, per),
        grid=(tiles + last,),
        in_specs=[pl.BlockSpec(o.shape, lambda i: (0, 0)) for o in outs]
        + [
            pl.BlockSpec((rows, experts), lambda i: (0, 0)),
            pl.BlockSpec((experts, lanes), lambda i: (0, 0)),
            keep,
            keep,
            pl.BlockSpec((WIDE, width), lambda i: (clamp(i), 0)),
            pl.BlockSpec((experts, WIDE, 2 * FF), lambda i: (0, later(i), 0)),
        ]
        + [pl.BlockSpec(memory_space=pl.ANY)] * len(held),
        out_specs=[
            pl.BlockSpec((rows, width), lambda i: (place, 0)),
            keep,
            keep,
            pl.BlockSpec((rows, lanes), lambda i: (0, 0)),
            pl.BlockSpec((rows, WIDE), lambda i: (0, later(i))),
        ],
        out_shape=[jax.ShapeDtypeStruct((total, width), jnp.bfloat16)]
        + [jax.ShapeDtypeStruct((total, hidden), jnp.bfloat16)] * 2
        + [
            jax.ShapeDtypeStruct((rows, lanes), jnp.float32),
            jax.ShapeDtypeStruct((rows, width), jnp.bfloat16),
        ],
        scratch_shapes=[pltpu.VMEM((rows, hidden), jnp.bfloat16)] * 2,
        input_output_aliases={known + i: i for i in range(len(held))},
        compiler_params=params(),
        cost_estimate=pl.CostEstimate(
            flops=6 * rows * hidden * width,
            bytes_accessed=6 * hidden * width + 12 * rows * width,
            transcendentals=rows * hidden,
        ),
        name="experts_backward",
    )(*outs, gates, own, gate, up, w_down, w_in, *held)


def ring_order(size):
    return list(range(0, size, 2)) + list(range(size - 1, 0, -2))


def ring_shift(rows, order, step):
    size = len(order)
    pairs = [(order[i], order[(i + step) % size]) for i in range(size)]
    return lax.ppermute(rows, "expert", pairs)


class Gather:
    def __init__(self, rows, order, name):
        self.order, self.half, self.done, self.name = order, len(order) // 2, 0, name
        self.blocks = {0: rows}

    def step(self, *waits):
        self.done = s = self.done + 1
        ahead, back = self.blocks[1 - s], self.blocks[s - 1]
        if s == self.half:
            cut = ahead.shape[0] // 2
            ahead, back = ahead[:cut], back[cut:]
        if waits:
            ahead, back = lax.optimization_barrier((ahead, back, *waits))[:2]
        with jax.named_scope(self.name):
            ahead, back = ring_shift(ahead, self.order, 1), ring_shift(back, self.order, -1)
        if s == self.half:
            self.parts = ahead, back
        else:
            self.blocks[-s], self.blocks[s] = ahead, back


    def join(self, *waits):
        parts = lax.optimization_barrier((*self.parts, *waits))[:2] if waits else self.parts
        self.blocks[self.half] = jnp.concatenate(parts, axis=0)


class Scatter:
    def __init__(self, far, order, name, *waits):
        self.order, self.cut, self.first, self.name = order, far.shape[0] // 2, True, name
        self.send(far[: self.cut], far[self.cut :], waits)

    def send(self, ahead, back, waits):
        ahead, back = ahead.astype(jnp.bfloat16), back.astype(jnp.bfloat16)
        if waits:
            ahead, back = lax.optimization_barrier((ahead, back, *waits))[:2]
        self.sent = (ahead, back)
        with jax.named_scope(self.name):
            self.ahead = ring_shift(ahead, self.order, 1).astype(jnp.float32)
            self.back = ring_shift(back, self.order, -1).astype(jnp.float32)

    def step(self, mine, other, *waits):
        mine, other = mine.astype(jnp.float32), other.astype(jnp.float32)
        if self.first:
            cut, self.first = self.cut, False
            mine = jnp.concatenate([mine[:cut] + self.ahead, mine[cut:]], axis=0)
            other = jnp.concatenate([other[:cut], other[cut:] + self.back], axis=0)
        else:
            mine, other = mine + self.ahead, other + self.back
        self.send(mine, other, waits)

    def finish(self, own):
        return own.astype(jnp.float32) + self.ahead + self.back


def offsets_of(size):
    half = size // 2
    out = [0]
    for step in range(1, half):
        out += [-step, step]
    return out + [half]


def sum_over(values, axis):
    size, step = lax.axis_size(axis), 1
    while step < size:
        values = values + lax.ppermute(values, axis, [(i, i ^ step) for i in range(size)])
        step *= 2
    return values


class Sum:
    def __init__(self, values):
        self.values = values
        self.left = [
            (axis, 1 << b)
            for axis in ("expert", "dp")
            for b in range(lax.axis_size(axis).bit_length() - 1)
        ]

    def step(self, *waits):
        if not self.left:
            return
        axis, bit = self.left.pop(0)
        values = after(self.values, *waits) if waits else self.values
        with jax.named_scope("sum_small"):
            other = lax.ppermute(values, axis, [(i, i ^ bit) for i in range(lax.axis_size(axis))])
        self.values = values + other

    def finish(self):
        while self.left:
            self.step()
        return self.values


def after(values, *others):
    return lax.optimization_barrier((values, *others))[0]


def weight_kernel(parts, adds, outs, index_ref, *refs):
    left_refs, right_ref, refs = refs[:parts], refs[parts], refs[parts + 1 :]
    add_refs, out_refs, left = refs[:adds], refs[adds : adds + outs], refs[-1]
    tile = left_refs[0].shape[1]

    @pl.when(pl.program_id(0) == 0)
    def _():
        for p, ref in enumerate(left_refs):
            left[p * tile : (p + 1) * tile, :] = ref[...].T

    total = dot_nn(left[...], right_ref[...])
    height = parts * tile // outs
    for o, out_ref in enumerate(out_refs):
        for p in range(parts // outs):
            at = o * height + p * tile
            part = total[at : at + tile]
            if adds:
                part = part + add_refs[at // tile][...].astype(jnp.float32)
            out_ref[p * tile : (p + 1) * tile, :] = part.astype(out_ref.dtype)


def weight_part(left, right, tile, columns, add, add_rows, types, name):
    rows, width, wide = left.shape[0], right.shape[1], WIDE
    parts, adds, outs = len(columns), len(add_rows), len(types)
    places = list(columns) + list(add_rows)
    height = parts * tile // outs
    in_specs = [
        pl.BlockSpec((rows, tile), lambda j, at, p=p: (0, at[p])) for p in range(parts)
    ] + [pl.BlockSpec((rows, wide), lambda j, at: (0, j))]
    in_specs += [
        pl.BlockSpec((tile, wide), lambda j, at, p=p: (at[p], j))
        for p in range(parts, len(places))
    ]
    return pl.pallas_call(
        functools.partial(weight_kernel, parts, adds, outs),
        grid_spec=pltpu.PrefetchScalarGridSpec(
            num_scalar_prefetch=1,
            grid=(width // wide,),
            in_specs=in_specs,
            out_specs=[pl.BlockSpec((height, wide), lambda j, at: (0, j))] * outs,
            scratch_shapes=[pltpu.VMEM((parts * tile, rows), jnp.bfloat16)],
        ),
        out_shape=[jax.ShapeDtypeStruct((height, width), t) for t in types],
        compiler_params=params(),
        cost_estimate=pl.CostEstimate(
            flops=2 * rows * parts * tile * width,
            bytes_accessed=2 * rows * (parts * tile + width) + 4 * parts * tile * width,
            transcendentals=0,
        ),
        name=name,
    )(jnp.stack([jnp.asarray(p, jnp.int32) for p in places]), *[left] * parts, right, *[add] * adds)


class GroupSum:
    def __init__(self, left, right, outer, name):
        self.left, self.right, self.outer, self.name = left, right, outer, name
        self.size = lax.axis_size("dp")
        me = lax.axis_index("dp")
        self.core, self.pair = me % 2, me // 2
        self.tile = left.shape[1] // outer // self.size

    def tiles(self, core, pairs):
        return [4 * o + 2 * pair + core for pair in pairs for o in range(self.outer)]

    def first(self, *waits):
        left = after(self.left, *waits) if waits else self.left
        if self.size != 4:
            terms = dot_tn(left, self.right).astype(jnp.bfloat16)
            terms = terms.reshape(self.outer, -1, terms.shape[1])
            self.far = self.near = lax.psum_scatter(terms, "dp", scatter_dimension=1, tiled=True)
            return
        columns = self.tiles(1 - self.core, (0, 1))
        (self.far,) = weight_part(
            left, self.right, self.tile, columns, None, [], [jnp.bfloat16], self.name
        )
        with jax.named_scope(self.name + "_cores"):
            self.got = lax.ppermute(self.far, "dp", [(i, i ^ 1) for i in range(4)])

    def second(self, *waits):
        if self.size != 4:
            return
        left = after(self.left, *waits) if waits else self.left
        pairs = (1 - self.pair, self.pair)
        self.near, self.own = weight_part(
            left,
            self.right,
            self.tile,
            self.tiles(self.core, pairs),
            self.got,
            [pair * self.outer + o for pair in pairs for o in range(self.outer)],
            [jnp.bfloat16, jnp.float32],
            self.name,
        )
        with jax.named_scope(self.name + "_groups"):
            self.back = lax.ppermute(self.near, "dp", [(i, i ^ 2) for i in range(4)])

    def total(self):
        if self.size != 4:
            return self.far.reshape(-1, self.far.shape[-1]).astype(jnp.float32)
        return self.own + self.back.astype(jnp.float32)


def body(
    tokens,
    lengths,
    routes,
    attn_gain,
    q_gain,
    k_gain,
    qkv_weight,
    out_weight,
    ffn_gain,
    router_weight,
    expert_in,
    expert_out,
    balance_coef,
    cotangent,
):
    bf16, f32 = jnp.bfloat16, jnp.float32
    n_expert = lax.axis_size("expert")
    group_index = lax.axis_index("dp")
    member = lax.axis_index("expert")
    slot_count = tokens.shape[1]
    seq_count = tokens.shape[2]
    width = tokens.shape[3]
    experts_here = expert_in.shape[0]
    experts_all = experts_here * n_expert
    tok_rows = slot_count * seq_count
    full_len = slot_count * n_expert
    heads_here = HEADS // n_expert
    cols = heads_here * HD

    order = ring_order(n_expert)
    offsets = offsets_of(n_expert)
    half = n_expert // 2
    table = [[order[(order.index(m) + r) % n_expert] for r in offsets] for m in range(n_expert)]
    owners = lax.dynamic_index_in_dim(jnp.array(table, jnp.int32), member, 0, False)
    owner = {r: owners[i] for i, r in enumerate(offsets)}

    def blockwise(blocks, axis=0):
        return jnp.concatenate([blocks[r] for r in offsets], axis=axis)

    def to_rows(values):
        return jnp.swapaxes(values[0], 0, 1).reshape(tok_rows, values.shape[3])

    def from_rows(rows):
        return jnp.swapaxes(rows.reshape(seq_count, slot_count, width), 0, 1)[None]

    seq_lens = lengths[group_index]
    slot_ids = member * slot_count + jnp.arange(slot_count)
    valid_rows = (slot_ids[None, :] < seq_lens[:, None]).astype(f32).reshape(tok_rows)
    all_slots = (owners[:, None] * slot_count + jnp.arange(slot_count)[None, :]).reshape(full_len)
    key_live = (all_slots[None, :] < seq_lens[:, None]).astype(f32)[:, None, :]
    inv_freq = jnp.exp(
        jnp.arange(HD // 2, dtype=f32) * (-2.0 * math.log(10000.0) / HD)
    )
    angles = all_slots.astype(f32)[:, None] * inv_freq[None, :]
    cosine, sine = jnp.cos(angles), jnp.sin(angles)
    cosine = jnp.concatenate([cosine, cosine], axis=1)
    sine = jnp.concatenate([-sine, sine], axis=1)
    head_gains = jnp.stack([q_gain, k_gain])

    inputs = to_rows(tokens).astype(f32)
    normed = norm_rows(inputs, attn_gain)

    lanes = 128
    picked_ids = to_rows(routes)
    chosen = jnp.sum(
        (picked_ids[:, :, None] == jnp.arange(experts_all)[None, None, :]).astype(f32), axis=1
    )
    hits = jnp.concatenate([chosen, valid_rows[:, None]], axis=1)
    hits = jnp.pad(hits, ((0, 0), (0, lanes - experts_all - 1)))
    normed_ring = Gather(
        jnp.concatenate([normed.astype(bf16), hits.astype(bf16)], axis=1), order, "ring_normed"
    )
    normed_ring.step()

    row_count = qkv_weight.shape[0]
    w_cols = qkv_weight.reshape(row_count, 3, n_expert, heads_here, HD).transpose(2, 0, 3, 1, 4)
    w_cols = lax.all_to_all(
        after(
            w_cols.reshape(n_expert, row_count, 3 * cols),
            normed_ring.blocks[1],
            normed_ring.blocks[-1],
        ),
        "expert",
        split_axis=0,
        concat_axis=0,
        tiled=True,
    )
    w_qkv = lax.all_gather(w_cols.reshape(-1, 3 * cols), "dp", axis=0, tiled=True)
    router_pad = jnp.pad(router_weight, ((0, 0), (0, lanes - experts_all)))
    own_ids = member * experts_here + jnp.arange(experts_here)
    own_rows = (own_ids[:, None] == jnp.arange(lanes)[None, :]).astype(f32)

    for _ in range(half - 2):
        normed_ring.step()
    w_out = lax.all_gather(
        after(out_weight, normed_ring.blocks[half - 1], normed_ring.blocks[1 - half]),
        "expert",
        axis=0,
        tiled=True,
    )
    normed_ring.step()
    normed_ring.join()
    hits_of = {r: normed_ring.blocks[r][:, width:] for r in offsets}
    normed_all = blockwise({r: normed_ring.blocks[r][:, :width] for r in offsets})
    hits_all = blockwise(hits_of).astype(f32)
    counts = jnp.sum(hits_all[:, experts_all : experts_all + 1] * hits_all, axis=0)
    count_total = sum_over(counts[:experts_all], "dp")
    n_valid = jnp.sum(lengths).astype(f32)
    fraction = count_total / (TOPK * n_valid)
    cot_rows = to_rows(cotangent)
    cot_ring = Gather(cot_rows, order, "ring_cotangent")
    cot_ring.step(normed_all)

    project = dot_nn(normed_all, w_qkv).reshape(n_expert, seq_count, slot_count, 3 * cols)
    attended = attend(owners, project, cosine, sine, key_live, head_gains)
    w_out = lax.all_gather(after(w_out, attended), "dp", axis=0, tiled=True)
    attended = after(attended, cot_ring.blocks[1], cot_ring.blocks[-1])
    cot_ring.step(attended)
    attended_low = lax.all_to_all(
        attended.reshape(n_expert, tok_rows, cols), "expert", split_axis=0, concat_axis=0, tiled=True
    )
    attended_low = jnp.swapaxes(attended_low, 0, 1).reshape(tok_rows, width)
    residual = inputs + dot_nn(attended_low, w_out)
    ffn_normed, ffn_back = jax.vjp(norm_rows, residual, ffn_gain)
    ffn_low = ffn_normed.astype(bf16)
    for _ in range(half - 3):
        cot_ring.step(residual)
    ffn_ring = Gather(ffn_low, order, "ring_ffn")
    ffn_ring.step()

    live = valid_rows[:, None]
    router_probs = jax.nn.softmax(dot_nn(ffn_low, router_weight), axis=-1)
    picked = chosen * router_probs
    picked_total = jnp.sum(picked, axis=-1, keepdims=True)
    prob_sums = jnp.sum(live * router_probs, axis=0)
    groups = [[0]] + [[-s, s] for s in range(1, half)] + [[half]]
    bases = [(n_expert - 2) * tok_rows]
    bases += [2 * s * tok_rows for s in range(half - 1)] + [(n_expert - 1) * tok_rows]
    w_down = expert_out.reshape(experts_here * FF, width)
    all_rows = n_expert * tok_rows

    def split(rows, group):
        return {r: rows[i * tok_rows : (i + 1) * tok_rows] for i, r in enumerate(group)}

    held, mix_blocks, group_gates = [], {}, []
    for i, g in enumerate(groups):
        *held, gates, mixed = experts_forward(
            [
                after(ffn_ring.blocks[r], cot_ring.blocks[half - 1], cot_ring.blocks[1 - half])
                if i == 2
                else ffn_ring.blocks[r]
                for r in g
            ],
            jnp.concatenate([hits_of[r] for r in g], axis=0),
            router_pad,
            own_rows,
            experts_all,
            expert_in,
            w_down,
            held,
            bases[i],
            all_rows,
        )
        group_gates.append(gates)
        mix_blocks.update(split(mixed, g))
        if i < half - 1:
            ffn_ring.step(mixed)
        if i == half - 1:
            ffn_ring.join()
        if i == 1:
            cot_ring.step(mixed)
    cot_ring.join(gates)
    x_all, gate_all, up_all, gated_all = held
    held, ffn_sum = [], None
    mix_sum = Scatter(mix_blocks[half], order, "ring_mixture")
    ready = ()
    for i in reversed(range(len(groups))):
        g = groups[i]
        *held, scores, grads = experts_backward(
            [cot_ring.blocks[r] for r in g],
            after(group_gates[i], *ready) if ready else group_gates[i],
            own_rows,
            gate_all,
            up_all,
            expert_in,
            w_down,
            held,
            bases[i],
        )
        grads = jnp.concatenate([grads, scores.astype(bf16)], axis=1)
        if i == half:
            ffn_sum = Scatter(grads, order, "ring_ffn_grad")
        elif i > 0:
            ffn_sum.step(grads[tok_rows:], grads[:tok_rows])
        if 2 < i < half:
            mix_sum.step(mix_blocks[i], mix_blocks[-i], grads)
        ready = (*mix_sum.sent, *ffn_sum.sent)
    out_all, gate_grad_all, up_grad_all = held
    sums = [
        GroupSum(gated_all, out_all, experts_here, "weights_out"),
        GroupSum(x_all, gate_grad_all, 1, "weights_gate"),
        GroupSum(x_all, up_grad_all, 1, "weights_up"),
    ]
    mix_sum.step(mix_blocks[2], mix_blocks[-2], grads)
    sums[0].first(*mix_sum.sent)
    ffn_grad = ffn_sum.finish(after(grads, sums[0].far))
    gate_grads = ffn_grad[:, width : width + experts_all] * chosen
    ffn_grad = ffn_grad[:, :width]
    picked_grad = (
        live
        * chosen
        * (
            gate_grads / picked_total
            - jnp.sum(gate_grads * picked, axis=-1, keepdims=True) / (picked_total * picked_total)
        )
    )
    prob_grad = picked_grad + balance_coef * experts_all * fraction[None, :] / n_valid * live
    logit_grad = router_probs * (
        prob_grad - jnp.sum(router_probs * prob_grad, axis=-1, keepdims=True)
    )
    ffn_grad = ffn_grad + jnp.dot(logit_grad, router_weight.astype(f32).T, precision=PRECISE)
    router_terms = jnp.dot(ffn_low.astype(f32).T, logit_grad, precision=PRECISE)
    residual_norm_grad, ffn_gain_terms = ffn_back(ffn_grad)
    residual_grad = cot_rows.astype(f32) * live + residual_norm_grad
    branch_grad = residual_grad.astype(bf16)

    attended_grad = dot_nt(branch_grad, w_out).astype(bf16)
    attended_grad = lax.all_to_all(
        jnp.swapaxes(attended_grad.reshape(tok_rows, n_expert, cols), 0, 1),
        "expert",
        split_axis=0,
        concat_axis=0,
        tiled=True,
    ).reshape(attended.shape)

    output_terms = dot_tn(attended_low, branch_grad).astype(bf16)
    out_share = lax.psum_scatter(output_terms, "dp", scatter_dimension=0, tiled=True)
    sums[0].second(branch_grad)
    attended_grad = after(attended_grad, sums[0].near, output_terms)

    mix_sum.step(mix_blocks[1], mix_blocks[-1], attended_grad)
    attended_grad = after(attended_grad, *mix_sum.sent)
    proj_grad, gain_parts = attend_back(
        owners, project, attended_grad, cosine, sine, key_live, head_gains
    )
    proj_grad = proj_grad.reshape(all_rows, 3 * cols)
    normed_terms = dot_nt(proj_grad, w_qkv).astype(bf16)
    block_rows = residual + mix_sum.finish(mix_blocks[0])
    normed_terms = after(normed_terms, block_rows)
    normed_parts = {
        r: normed_terms[i * tok_rows : (i + 1) * tok_rows] for i, r in enumerate(offsets)
    }
    normed_sum = Scatter(normed_parts[half], order, "ring_normed_grad")
    attn_gain_terms = (
        jnp.sum(normed_terms.astype(f32) * normed_all.astype(f32), axis=0) / attn_gain
    )
    head_gain_grads = jnp.sum(gain_parts, axis=(0, 1)).reshape(-1)
    small = Sum(
        jnp.concatenate(
            [
                router_terms.reshape(-1),
                ffn_gain_terms,
                attn_gain_terms,
                head_gain_grads,
                prob_sums,
            ]
        )
    )
    sums[1].first(normed_terms)
    waits = [sums[1].far]
    for s in range(half - 1, 0, -1):
        normed_sum.step(normed_parts[s], normed_parts[-s], *waits)
        waits = []
        if s == half - 1:
            sums[1].second(normed_terms)
            proj_terms = dot_tn(after(normed_all, sums[1].near), proj_grad).astype(bf16)
            waits = [sums[1].near, proj_terms]
        if s == half - 2:
            sums[2].first(proj_terms)
            waits = [sums[2].far]
        if s == half - 3:
            sums[2].second(proj_terms)
    proj_share = lax.psum_scatter(proj_terms, "dp", scatter_dimension=0, tiled=True)
    normed_grad = normed_sum.finish(after(normed_parts[0], sums[2].near))
    grad_out = lax.psum_scatter(
        out_share, "expert", scatter_dimension=0, tiled=True
    ).astype(f32)
    (input_norm_grad,) = jax.vjp(lambda v: norm_rows(v, attn_gain), inputs)[1](normed_grad)
    grad_tokens = from_rows(residual_grad + input_norm_grad)
    block_out = from_rows(block_rows)
    grad_expert_out = sums[0].total().reshape(experts_here, -1, width)
    shares = [sums[1].total(), sums[2].total()]
    grad_expert_in = jnp.stack(
        [
            jnp.concatenate([s[:, e * FF : (e + 1) * FF] for s in shares], axis=1)
            for e in range(experts_here)
        ]
    )

    grad_qkv = lax.all_to_all(
        proj_share.reshape(n_expert, row_count, 3 * cols),
        "expert",
        split_axis=0,
        concat_axis=0,
        tiled=True,
    ).reshape(n_expert, row_count, heads_here, 3, HD)
    grad_qkv = grad_qkv.transpose(1, 3, 0, 2, 4).reshape(row_count, 3, width).astype(f32)

    small.step(normed_grad)
    small.step(grad_qkv)
    small = small.finish()
    places, pieces = 0, []
    for size in (width * experts_all, width, width, HD, HD, experts_all):
        pieces.append(small[places : places + size])
        places += size
    grad_router, grad_ffn_gain, grad_attn_gain, grad_q_gain, grad_k_gain, prob_total = pieces
    balance_loss = balance_coef * experts_all * jnp.sum(fraction * (prob_total / n_valid))
    return (
        block_out,
        balance_loss,
        grad_tokens,
        grad_attn_gain,
        grad_q_gain,
        grad_k_gain,
        grad_qkv,
        grad_out,
        grad_ffn_gain,
        grad_router.reshape(width, experts_all),
        grad_expert_in,
        grad_expert_out,
    )


def solution(mesh):
    placed = (
        P("dp", "expert", None, None),
        P(),
        P("dp", "expert", None, None),
        P(),
        P(),
        P(),
        P(("dp", "expert"), None, None),
        P(("dp", "expert"), None),
        P(),
        P(),
        P("expert", None, None),
        P("expert", None, None),
        P(),
        P("dp", "expert", None, None),
    )
    return jax.shard_map(
        body,
        mesh=mesh,
        in_specs=placed,
        out_specs=(
            P("dp", "expert", None, None),
            P(),
            P("dp", "expert", None, None),
            P(),
            P(),
            P(),
            P(("dp", "expert"), None, None),
            P(("dp", "expert"), None),
            P(),
            P(),
            P("expert", "dp", None),
            P("expert", "dp", None),
        ),
        check_vma=False,
    )
```

```python
import functools
import math

import jax
import jax.numpy as jnp
from jax import lax
from jax.experimental import pallas as pl
from jax.experimental.pallas import tpu as pltpu
from jax.sharding import PartitionSpec as P

HEADS = 16
HD = 128
FF = 1024
TOPK = 8


NORM_EPS = 1e-05
PRECISE = lax.Precision.HIGHEST


def norm_rows(values, scale_gain):
    return (
        values
        * lax.rsqrt(jnp.mean(values * values, axis=-1, keepdims=True) + NORM_EPS)
        * scale_gain
    )


VMEM_BYTES = 56 * 1024 * 1024
TILE = 256
WIDE = 512


def params():
    return pltpu.CompilerParams(vmem_limit_bytes=VMEM_BYTES)


def dot_nn(left, right):
    return jnp.dot(left, right, preferred_element_type=jnp.float32)


def dot_nt(left, right):
    return lax.dot_general(
        left, right, (((1,), (1,)), ((), ())), preferred_element_type=jnp.float32
    )


def dot_tn(left, right):
    return lax.dot_general(
        left, right, (((0,), (0,)), ((), ())), preferred_element_type=jnp.float32
    )


def turn(values, cosine, sine):
    return values * cosine + pltpu.roll(values, HD // 2, 1) * sine


def turn_back(values, cosine, sine):
    return values * cosine + pltpu.roll(values * sine, HD // 2, 1)


def head_norm(proj):
    return lax.rsqrt(jnp.mean(proj * proj, axis=-1, keepdims=True) + NORM_EPS)


def load_heads(proj_ref, cos_ref, sin_ref, gain_ref):
    rows = cos_ref.shape[0]
    proj = proj_ref[...].reshape(rows, 3 * HD)
    cosine, sine = cos_ref[...], sin_ref[...]
    q_proj, k_proj, v_proj = proj[:, :HD], proj[:, HD : 2 * HD], proj[:, 2 * HD :]
    queries = turn(q_proj * head_norm(q_proj) * gain_ref[0:1], cosine, sine).astype(jnp.bfloat16)
    keys = turn(k_proj * head_norm(k_proj) * gain_ref[1:2], cosine, sine).astype(jnp.bfloat16)
    return q_proj, k_proj, queries, keys, v_proj.astype(jnp.bfloat16)


def row_probs(queries, keys, live):
    scores = jnp.where(live, dot_nt(queries, keys), -1e30)
    expo = jnp.exp((scores - jnp.max(scores, axis=-1, keepdims=True)) * (1.0 / math.sqrt(HD)))
    return expo * (1.0 / jnp.sum(expo, axis=-1, keepdims=True))


def attend_kernel(
    owner_ref, proj_ref, cos_ref, sin_ref, live_ref, gain_ref, out_ref, q_scr, o_scr
):
    rows, slots = cos_ref.shape[0], proj_ref.shape[2]
    step = min(WIDE, rows)
    _, _, queries, keys, values = load_heads(proj_ref, cos_ref, sin_ref, gain_ref)
    q_scr[...] = queries
    live = live_ref[0] > 0.0

    def chunk(i, carry):
        part = pl.ds(pl.multiple_of(i * step, step), step)
        probs = row_probs(q_scr[part, :], keys, live).astype(jnp.bfloat16)
        o_scr[part, :] = dot_nn(probs, values).astype(jnp.bfloat16)
        return carry

    lax.fori_loop(0, rows // step, chunk, 0, unroll=True)
    for r in range(proj_ref.shape[0]):
        out_ref[owner_ref[r], 0] = o_scr[r * slots : (r + 1) * slots, :]


def attend(owners, proj, cosine, sine, live, gains):
    blocks, seqs, slots, width = proj.shape
    heads, rows = width // (3 * HD), blocks * slots
    return pl.pallas_call(
        attend_kernel,
        grid_spec=pltpu.PrefetchScalarGridSpec(
            num_scalar_prefetch=1,
            grid=(seqs, heads),
            in_specs=[
                pl.BlockSpec((blocks, 1, slots, 3 * HD), lambda s, h, o: (0, s, 0, h)),
                pl.BlockSpec((rows, HD), lambda s, h, o: (0, 0)),
                pl.BlockSpec((rows, HD), lambda s, h, o: (0, 0)),
                pl.BlockSpec((1, 1, rows), lambda s, h, o: (s, 0, 0)),
                pl.BlockSpec((2, HD), lambda s, h, o: (0, 0)),
            ],
            out_specs=pl.BlockSpec((blocks, 1, slots, HD), lambda s, h, o: (0, s, 0, h)),
            scratch_shapes=[pltpu.VMEM((rows, HD), jnp.bfloat16)] * 2,
        ),
        out_shape=jax.ShapeDtypeStruct((blocks, seqs, slots, heads * HD), jnp.bfloat16),
        compiler_params=params(),
        cost_estimate=pl.CostEstimate(
            flops=4 * seqs * heads * rows * rows * HD,
            bytes_accessed=seqs * rows * width * 5,
            transcendentals=seqs * heads * rows * rows,
        ),
        name="attend",
    )(owners, proj, cosine, sine, live, gains)


def attend_back_kernel(
    owner_ref, proj_ref, grad_ref, cos_ref, sin_ref, live_ref, gain_ref, out_ref, gain_out, q_scr, dq, dk, dv
):
    rows, slots = cos_ref.shape[0], proj_ref.shape[2]
    step = min(WIDE, rows)
    scale = 1.0 / math.sqrt(HD)
    q_proj, k_proj, queries, keys, values = load_heads(proj_ref, cos_ref, sin_ref, gain_ref)
    q_scr[0] = queries
    for r in range(proj_ref.shape[0]):
        q_scr[1, r * slots : (r + 1) * slots, :] = grad_ref[owner_ref[r], 0]
    dk[...] = jnp.zeros_like(dk)
    dv[...] = jnp.zeros_like(dv)
    live = live_ref[0] > 0.0

    def chunk(i, carry):
        part = pl.ds(pl.multiple_of(i * step, step), step)
        q_part, g_part = q_scr[0, part, :], q_scr[1, part, :]
        probs = row_probs(q_part, keys, live)
        prob_grad = dot_nt(g_part, values)
        row_dot = jnp.sum(probs * prob_grad, axis=-1, keepdims=True)
        score_grad = (probs * (prob_grad - row_dot)).astype(jnp.bfloat16)
        dq[part, :] = dot_nn(score_grad, keys)
        dk[...] += dot_tn(score_grad, q_part)
        dv[...] += dot_tn(probs.astype(jnp.bfloat16), g_part)
        return carry

    lax.fori_loop(0, rows // step, chunk, 0, unroll=True)
    cosine, sine = cos_ref[...], sin_ref[...]
    parts = []
    for i, (proj, grad) in enumerate(((q_proj, dq), (k_proj, dk))):
        gain, inverse = gain_ref[i : i + 1], head_norm(proj)
        back = turn_back(grad[...] * scale, cosine, sine)
        scaled = proj * inverse
        gain_out[0, 0, i : i + 1, :] = jnp.sum(back * scaled, axis=0, keepdims=True)
        back = back * gain
        parts.append(
            inverse * (back - scaled * jnp.mean(scaled * back, axis=-1, keepdims=True))
        )
    grads = jnp.concatenate(parts + [dv[...]], axis=1).astype(jnp.bfloat16)
    out_ref[...] = grads.reshape(out_ref.shape)


def attend_back(owners, proj, grads, cosine, sine, live, gains):
    blocks, seqs, slots, width = proj.shape
    heads, rows = width // (3 * HD), blocks * slots
    return pl.pallas_call(
        attend_back_kernel,
        grid_spec=pltpu.PrefetchScalarGridSpec(
            num_scalar_prefetch=1,
            grid=(seqs, heads),
            in_specs=[
                pl.BlockSpec((blocks, 1, slots, 3 * HD), lambda s, h, o: (0, s, 0, h)),
                pl.BlockSpec((blocks, 1, slots, HD), lambda s, h, o: (0, s, 0, h)),
                pl.BlockSpec((rows, HD), lambda s, h, o: (0, 0)),
                pl.BlockSpec((rows, HD), lambda s, h, o: (0, 0)),
                pl.BlockSpec((1, 1, rows), lambda s, h, o: (s, 0, 0)),
                pl.BlockSpec((2, HD), lambda s, h, o: (0, 0)),
            ],
            out_specs=[
                pl.BlockSpec((blocks, 1, slots, 3 * HD), lambda s, h, o: (0, s, 0, h)),
                pl.BlockSpec((1, 1, 2, HD), lambda s, h, o: (s, h, 0, 0)),
            ],
            scratch_shapes=[pltpu.VMEM((2, rows, HD), jnp.bfloat16)]
            + [pltpu.VMEM((rows, HD), jnp.float32)] * 3,
        ),
        out_shape=[
            jax.ShapeDtypeStruct(proj.shape, jnp.bfloat16),
            jax.ShapeDtypeStruct((seqs, heads, 2, HD), jnp.float32),
        ],
        compiler_params=params(),
        cost_estimate=pl.CostEstimate(
            flops=10 * seqs * heads * rows * rows * HD,
            bytes_accessed=seqs * rows * width * 7,
            transcendentals=seqs * heads * rows * rows,
        ),
        name="attend_back",
    )(owners, proj, grads, cosine, sine, live, gains)


def gate_column(gates_ref, index):
    gates = gates_ref[...]
    out = jnp.zeros((gates.shape[0], 1), jnp.float32)
    for e in range(gates.shape[1]):
        out = out + jnp.where(index == e, gates[:, e : e + 1], 0.0)
    return out


def fill_rows(refs, out_ref):
    base = 0
    for ref in refs:
        out_ref[base : base + ref.shape[0], :] = ref[...]
        base += ref.shape[0]


def experts_kernel(parts, held, tiles, per, count, *refs):
    x_refs, refs = refs[:parts], refs[parts:]
    hits_ref, router_ref, own_ref, gate_w, up_w, down_w = refs[:6]
    rows, gate_out, up_out, gated_out, gates_ref, mix_out, gated = refs[6 + held :]
    i = pl.program_id(0)

    @pl.when(i == 0)
    def _():
        fill_rows(x_refs, rows)
        logits = dot_nn(rows[...], router_ref[...])
        hits = hits_ref[...].astype(jnp.float32)
        lane = lax.broadcasted_iota(jnp.int32, logits.shape, 1)
        logits = jnp.where(lane < count, logits, -1e30)
        expo = jnp.exp(logits - jnp.max(logits, axis=1, keepdims=True))
        picked = jnp.where(lane < count, hits * expo / jnp.sum(expo, axis=1, keepdims=True), 0.0)
        live = jnp.sum(jnp.where(lane == count, hits, 0.0), axis=1, keepdims=True)
        gates = live * picked / jnp.sum(picked, axis=1, keepdims=True)
        for e in range(gates_ref.shape[1]):
            gates_ref[:, e : e + 1] = jnp.sum(gates * own_ref[e : e + 1], axis=1, keepdims=True)

    @pl.when(i < tiles)
    def _():
        gate = dot_nn(rows[...], gate_w[0])
        up = dot_nn(rows[...], up_w[0])
        hidden = gate / (1.0 + jnp.exp(-gate)) * up * gate_column(gates_ref, i // per)
        gate_out[...] = gate.astype(jnp.bfloat16)
        up_out[...] = up.astype(jnp.bfloat16)
        low = hidden.astype(jnp.bfloat16)
        gated_out[...] = low
        gated[:, pl.ds(pl.multiple_of(i * WIDE, WIDE), WIDE)] = low

    @pl.when(i >= tiles)
    def _():
        mix_out[...] = dot_nn(gated[...], down_w[...]).astype(jnp.bfloat16)


def experts_forward(xs, hits, router, own, count, w_in, w_down, held, base, total):
    experts, width, _ = w_in.shape
    hidden = w_down.shape[0]
    rows = sum(x.shape[0] for x in xs)
    place = base // rows
    tiles, per, outs = hidden // WIDE, FF // WIDE, width // WIDE
    clamp = lambda i: jnp.minimum(i, tiles - 1)
    later = lambda i: jnp.maximum(i - tiles, 0)
    keep = pl.BlockSpec((rows, WIDE), lambda i: (place, clamp(i)))
    known = len(xs) + 6
    lanes = router.shape[1]
    return pl.pallas_call(
        functools.partial(experts_kernel, len(xs), len(held), tiles, per, count),
        grid=(tiles + outs,),
        in_specs=[pl.BlockSpec(x.shape, lambda i: (0, 0)) for x in xs]
        + [
            pl.BlockSpec((rows, lanes), lambda i: (0, 0)),
            pl.BlockSpec((width, lanes), lambda i: (0, 0)),
            pl.BlockSpec((experts, lanes), lambda i: (0, 0)),
            pl.BlockSpec((1, width, WIDE), lambda i: (clamp(i) // per, 0, clamp(i) % per)),
            pl.BlockSpec((1, width, WIDE), lambda i: (clamp(i) // per, 0, per + clamp(i) % per)),
            pl.BlockSpec((hidden, WIDE), lambda i: (0, later(i))),
        ]
        + [pl.BlockSpec(memory_space=pl.ANY)] * len(held),
        out_specs=[pl.BlockSpec((rows, width), lambda i: (place, 0))]
        + [keep] * 3
        + [
            pl.BlockSpec((rows, experts), lambda i: (0, 0)),
            pl.BlockSpec((rows, WIDE), lambda i: (0, later(i))),
        ],
        out_shape=[jax.ShapeDtypeStruct((total, width), jnp.bfloat16)]
        + [jax.ShapeDtypeStruct((total, hidden), jnp.bfloat16)] * 3
        + [
            jax.ShapeDtypeStruct((rows, experts), jnp.float32),
            jax.ShapeDtypeStruct((rows, width), jnp.bfloat16),
        ],
        scratch_shapes=[pltpu.VMEM((rows, hidden), jnp.bfloat16)],
        input_output_aliases={known + i: i for i in range(len(held))},
        compiler_params=params(),
        cost_estimate=pl.CostEstimate(
            flops=6 * rows * hidden * width,
            bytes_accessed=6 * hidden * width + 10 * rows * width,
            transcendentals=rows * hidden,
        ),
        name="experts_forward",
    )(*xs, hits, router, own, w_in, w_in, w_down, *held)


def experts_back_kernel(parts, held, tiles, per, *refs):
    c_refs, refs = refs[:parts], refs[parts:]
    gates_ref, own_ref, gate_ref, up_ref, down_w, in_w = refs[:6]
    rows, gate_out, up_out, score_out, grad_out, gate_grads, up_grads = refs[6 + held :]
    i = pl.program_id(0)

    @pl.when(i == 0)
    def _():
        fill_rows(c_refs, rows)

    @pl.when(i < tiles)
    def _():
        raw = dot_nt(rows[...], down_w[...])
        gate, up = gate_ref[...].astype(jnp.float32), up_ref[...].astype(jnp.float32)
        sigmoid = 1.0 / (1.0 + jnp.exp(-gate))
        silu = gate * sigmoid
        score = jnp.sum(silu * up * raw, axis=1, keepdims=True)
        own = own_ref[...]
        place = sum(jnp.where(i // per == e, own[e : e + 1], 0.0) for e in range(own.shape[0]))
        mine = score * place
        score_out[...] = jnp.where(i == 0, mine, score_out[...] + mine)
        grad = raw * gate_column(gates_ref, i // per)
        gate_low = (grad * up * (sigmoid + silu * (1.0 - sigmoid))).astype(jnp.bfloat16)
        up_low = (grad * silu).astype(jnp.bfloat16)
        gate_out[...] = gate_low
        up_out[...] = up_low
        part = pl.ds(pl.multiple_of(i * WIDE, WIDE), WIDE)
        gate_grads[:, part] = gate_low
        up_grads[:, part] = up_low

    @pl.when(i >= tiles)
    def _():
        total = 0.0
        for e in range(in_w.shape[0]):
            part = slice(e * FF, (e + 1) * FF)
            total = total + dot_nt(gate_grads[:, part], in_w[e, :, :FF])
            total = total + dot_nt(up_grads[:, part], in_w[e, :, FF:])
        grad_out[...] = total.astype(jnp.bfloat16)


def experts_backward(outs, gates, own, gate, up, w_in, w_down, held, base):
    experts, width, _ = w_in.shape
    hidden, total = w_down.shape[0], gate.shape[0]
    rows = sum(o.shape[0] for o in outs)
    place = base // rows
    tiles, per, last = hidden // WIDE, FF // WIDE, width // WIDE
    clamp = lambda i: jnp.minimum(i, tiles - 1)
    later = lambda i: jnp.maximum(i - tiles, 0)
    keep = pl.BlockSpec((rows, WIDE), lambda i: (place, clamp(i)))
    known, lanes = len(outs) + 6, own.shape[1]
    return pl.pallas_call(
        functools.partial(experts_back_kernel, len(outs), len(held), tiles, per),
        grid=(tiles + last,),
        in_specs=[pl.BlockSpec(o.shape, lambda i: (0, 0)) for o in outs]
        + [
            pl.BlockSpec((rows, experts), lambda i: (0, 0)),
            pl.BlockSpec((experts, lanes), lambda i: (0, 0)),
            keep,
            keep,
            pl.BlockSpec((WIDE, width), lambda i: (clamp(i), 0)),
            pl.BlockSpec((experts, WIDE, 2 * FF), lambda i: (0, later(i), 0)),
        ]
        + [pl.BlockSpec(memory_space=pl.ANY)] * len(held),
        out_specs=[
            pl.BlockSpec((rows, width), lambda i: (place, 0)),
            keep,
            keep,
            pl.BlockSpec((rows, lanes), lambda i: (0, 0)),
            pl.BlockSpec((rows, WIDE), lambda i: (0, later(i))),
        ],
        out_shape=[jax.ShapeDtypeStruct((total, width), jnp.bfloat16)]
        + [jax.ShapeDtypeStruct((total, hidden), jnp.bfloat16)] * 2
        + [
            jax.ShapeDtypeStruct((rows, lanes), jnp.float32),
            jax.ShapeDtypeStruct((rows, width), jnp.bfloat16),
        ],
        scratch_shapes=[pltpu.VMEM((rows, hidden), jnp.bfloat16)] * 2,
        input_output_aliases={known + i: i for i in range(len(held))},
        compiler_params=params(),
        cost_estimate=pl.CostEstimate(
            flops=6 * rows * hidden * width,
            bytes_accessed=6 * hidden * width + 12 * rows * width,
            transcendentals=rows * hidden,
        ),
        name="experts_backward",
    )(*outs, gates, own, gate, up, w_down, w_in, *held)


def ring_order(size):
    return list(range(0, size, 2)) + list(range(size - 1, 0, -2))


def ring_shift(rows, order, step):
    size = len(order)
    pairs = [(order[i], order[(i + step) % size]) for i in range(size)]
    return lax.ppermute(rows, "expert", pairs)


class Gather:
    def __init__(self, rows, order, name):
        self.order, self.half, self.done, self.name = order, len(order) // 2, 0, name
        self.blocks = {0: rows}

    def step(self, *waits):
        self.done = s = self.done + 1
        ahead, back = self.blocks[1 - s], self.blocks[s - 1]
        if s == self.half:
            cut = ahead.shape[0] // 2
            ahead, back = ahead[:cut], back[cut:]
        if waits:
            ahead, back = lax.optimization_barrier((ahead, back, *waits))[:2]
        with jax.named_scope(self.name):
            ahead, back = ring_shift(ahead, self.order, 1), ring_shift(back, self.order, -1)
        if s == self.half:
            self.parts = ahead, back
        else:
            self.blocks[-s], self.blocks[s] = ahead, back


    def join(self, *waits):
        parts = lax.optimization_barrier((*self.parts, *waits))[:2] if waits else self.parts
        self.blocks[self.half] = jnp.concatenate(parts, axis=0)


class Scatter:
    def __init__(self, far, order, name, *waits):
        self.order, self.cut, self.first, self.name = order, far.shape[0] // 2, True, name
        self.send(far[: self.cut], far[self.cut :], waits)

    def send(self, ahead, back, waits):
        ahead, back = ahead.astype(jnp.bfloat16), back.astype(jnp.bfloat16)
        if waits:
            ahead, back = lax.optimization_barrier((ahead, back, *waits))[:2]
        self.sent = (ahead, back)
        with jax.named_scope(self.name):
            self.ahead = ring_shift(ahead, self.order, 1).astype(jnp.float32)
            self.back = ring_shift(back, self.order, -1).astype(jnp.float32)

    def step(self, mine, other, *waits):
        mine, other = mine.astype(jnp.float32), other.astype(jnp.float32)
        if self.first:
            cut, self.first = self.cut, False
            mine = jnp.concatenate([mine[:cut] + self.ahead, mine[cut:]], axis=0)
            other = jnp.concatenate([other[:cut], other[cut:] + self.back], axis=0)
        else:
            mine, other = mine + self.ahead, other + self.back
        self.send(mine, other, waits)

    def finish(self, own):
        return own.astype(jnp.float32) + self.ahead + self.back


def offsets_of(size):
    half = size // 2
    out = [0]
    for step in range(1, half):
        out += [-step, step]
    return out + [half]


def sum_over(values, axis):
    size, step = lax.axis_size(axis), 1
    while step < size:
        values = values + lax.ppermute(values, axis, [(i, i ^ step) for i in range(size)])
        step *= 2
    return values


class Sum:
    def __init__(self, values):
        self.values = values
        self.left = [
            (axis, 1 << b)
            for axis in ("expert", "dp")
            for b in range(lax.axis_size(axis).bit_length() - 1)
        ]

    def step(self, *waits):
        if not self.left:
            return
        axis, bit = self.left.pop(0)
        values = after(self.values, *waits) if waits else self.values
        with jax.named_scope("sum_small"):
            other = lax.ppermute(values, axis, [(i, i ^ bit) for i in range(lax.axis_size(axis))])
        self.values = values + other

    def finish(self):
        while self.left:
            self.step()
        return self.values


def after(values, *others):
    return lax.optimization_barrier((values, *others))[0]


def weight_kernel(parts, adds, outs, index_ref, *refs):
    left_refs, right_ref, refs = refs[:parts], refs[parts], refs[parts + 1 :]
    add_refs, out_refs, left = refs[:adds], refs[adds : adds + outs], refs[-1]
    tile = left_refs[0].shape[1]

    @pl.when(pl.program_id(0) == 0)
    def _():
        for p, ref in enumerate(left_refs):
            left[p * tile : (p + 1) * tile, :] = ref[...].T

    total = dot_nn(left[...], right_ref[...])
    height = parts * tile // outs
    for o, out_ref in enumerate(out_refs):
        for p in range(parts // outs):
            at = o * height + p * tile
            part = total[at : at + tile]
            if adds:
                part = part + add_refs[at // tile][...].astype(jnp.float32)
            out_ref[p * tile : (p + 1) * tile, :] = part.astype(out_ref.dtype)


def weight_part(left, right, tile, columns, add, add_rows, types, name):
    rows, width, wide = left.shape[0], right.shape[1], WIDE
    parts, adds, outs = len(columns), len(add_rows), len(types)
    places = list(columns) + list(add_rows)
    height = parts * tile // outs
    in_specs = [
        pl.BlockSpec((rows, tile), lambda j, at, p=p: (0, at[p])) for p in range(parts)
    ] + [pl.BlockSpec((rows, wide), lambda j, at: (0, j))]
    in_specs += [
        pl.BlockSpec((tile, wide), lambda j, at, p=p: (at[p], j))
        for p in range(parts, len(places))
    ]
    return pl.pallas_call(
        functools.partial(weight_kernel, parts, adds, outs),
        grid_spec=pltpu.PrefetchScalarGridSpec(
            num_scalar_prefetch=1,
            grid=(width // wide,),
            in_specs=in_specs,
            out_specs=[pl.BlockSpec((height, wide), lambda j, at: (0, j))] * outs,
            scratch_shapes=[pltpu.VMEM((parts * tile, rows), jnp.bfloat16)],
        ),
        out_shape=[jax.ShapeDtypeStruct((height, width), t) for t in types],
        compiler_params=params(),
        cost_estimate=pl.CostEstimate(
            flops=2 * rows * parts * tile * width,
            bytes_accessed=2 * rows * (parts * tile + width) + 4 * parts * tile * width,
            transcendentals=0,
        ),
        name=name,
    )(jnp.stack([jnp.asarray(p, jnp.int32) for p in places]), *[left] * parts, right, *[add] * adds)


class GroupSum:
    def __init__(self, left, right, outer, name):
        self.left, self.right, self.outer, self.name = left, right, outer, name
        self.size = lax.axis_size("dp")
        me = lax.axis_index("dp")
        self.core, self.pair = me % 2, me // 2
        self.tile = left.shape[1] // outer // self.size

    def tiles(self, core, pairs):
        return [4 * o + 2 * pair + core for pair in pairs for o in range(self.outer)]

    def first(self, *waits):
        left = after(self.left, *waits) if waits else self.left
        if self.size != 4:
            terms = dot_tn(left, self.right).astype(jnp.bfloat16)
            terms = terms.reshape(self.outer, -1, terms.shape[1])
            self.far = self.near = lax.psum_scatter(terms, "dp", scatter_dimension=1, tiled=True)
            return
        columns = self.tiles(1 - self.core, (0, 1))
        (self.far,) = weight_part(
            left, self.right, self.tile, columns, None, [], [jnp.bfloat16], self.name
        )
        with jax.named_scope(self.name + "_cores"):
            self.got = lax.ppermute(self.far, "dp", [(i, i ^ 1) for i in range(4)])

    def second(self, *waits):
        if self.size != 4:
            return
        left = after(self.left, *waits) if waits else self.left
        pairs = (1 - self.pair, self.pair)
        self.near, self.own = weight_part(
            left,
            self.right,
            self.tile,
            self.tiles(self.core, pairs),
            self.got,
            [pair * self.outer + o for pair in pairs for o in range(self.outer)],
            [jnp.bfloat16, jnp.float32],
            self.name,
        )
        with jax.named_scope(self.name + "_groups"):
            self.back = lax.ppermute(self.near, "dp", [(i, i ^ 2) for i in range(4)])

    def total(self):
        if self.size != 4:
            return self.far.reshape(-1, self.far.shape[-1]).astype(jnp.float32)
        return self.own + self.back.astype(jnp.float32)


def body(
    tokens,
    lengths,
    routes,
    attn_gain,
    q_gain,
    k_gain,
    qkv_weight,
    out_weight,
    ffn_gain,
    router_weight,
    expert_in,
    expert_out,
    balance_coef,
    cotangent,
):
    bf16, f32 = jnp.bfloat16, jnp.float32
    n_expert = lax.axis_size("expert")
    group_index = lax.axis_index("dp")
    member = lax.axis_index("expert")
    slot_count = tokens.shape[1]
    seq_count = tokens.shape[2]
    width = tokens.shape[3]
    experts_here = expert_in.shape[0]
    experts_all = experts_here * n_expert
    tok_rows = slot_count * seq_count
    full_len = slot_count * n_expert
    heads_here = HEADS // n_expert
    cols = heads_here * HD

    order = ring_order(n_expert)
    offsets = offsets_of(n_expert)
    half = n_expert // 2
    table = [[order[(order.index(m) + r) % n_expert] for r in offsets] for m in range(n_expert)]
    owners = lax.dynamic_index_in_dim(jnp.array(table, jnp.int32), member, 0, False)
    owner = {r: owners[i] for i, r in enumerate(offsets)}

    def blockwise(blocks, axis=0):
        return jnp.concatenate([blocks[r] for r in offsets], axis=axis)

    def to_rows(values):
        return jnp.swapaxes(values[0], 0, 1).reshape(tok_rows, values.shape[3])

    def from_rows(rows):
        return jnp.swapaxes(rows.reshape(seq_count, slot_count, width), 0, 1)[None]

    seq_lens = lengths[group_index]
    slot_ids = member * slot_count + jnp.arange(slot_count)
    valid_rows = (slot_ids[None, :] < seq_lens[:, None]).astype(f32).reshape(tok_rows)
    all_slots = (owners[:, None] * slot_count + jnp.arange(slot_count)[None, :]).reshape(full_len)
    key_live = (all_slots[None, :] < seq_lens[:, None]).astype(f32)[:, None, :]
    inv_freq = jnp.exp(
        jnp.arange(HD // 2, dtype=f32) * (-2.0 * math.log(10000.0) / HD)
    )
    angles = all_slots.astype(f32)[:, None] * inv_freq[None, :]
    cosine, sine = jnp.cos(angles), jnp.sin(angles)
    cosine = jnp.concatenate([cosine, cosine], axis=1)
    sine = jnp.concatenate([-sine, sine], axis=1)
    head_gains = jnp.stack([q_gain, k_gain])

    inputs = to_rows(tokens).astype(f32)
    normed = norm_rows(inputs, attn_gain)

    lanes = 128
    picked_ids = to_rows(routes)
    chosen = jnp.sum(
        (picked_ids[:, :, None] == jnp.arange(experts_all)[None, None, :]).astype(f32), axis=1
    )
    hits = jnp.concatenate([chosen, valid_rows[:, None]], axis=1)
    hits = jnp.pad(hits, ((0, 0), (0, lanes - experts_all - 1)))
    normed_ring = Gather(
        jnp.concatenate([normed.astype(bf16), hits.astype(bf16)], axis=1), order, "ring_normed"
    )
    normed_ring.step()

    row_count = qkv_weight.shape[0]
    w_cols = qkv_weight.reshape(row_count, 3, n_expert, heads_here, HD).transpose(2, 0, 3, 1, 4)
    w_cols = lax.all_to_all(
        after(
            w_cols.reshape(n_expert, row_count, 3 * cols),
            normed_ring.blocks[1],
            normed_ring.blocks[-1],
        ),
        "expert",
        split_axis=0,
        concat_axis=0,
        tiled=True,
    )
    w_qkv = lax.all_gather(w_cols.reshape(-1, 3 * cols), "dp", axis=0, tiled=True)
    router_pad = jnp.pad(router_weight, ((0, 0), (0, lanes - experts_all)))
    own_ids = member * experts_here + jnp.arange(experts_here)
    own_rows = (own_ids[:, None] == jnp.arange(lanes)[None, :]).astype(f32)

    for _ in range(half - 2):
        normed_ring.step()
    w_out = lax.all_gather(
        after(out_weight, normed_ring.blocks[half - 1], normed_ring.blocks[1 - half]),
        "expert",
        axis=0,
        tiled=True,
    )
    normed_ring.step()
    normed_ring.join()
    hits_of = {r: normed_ring.blocks[r][:, width:] for r in offsets}
    normed_all = blockwise({r: normed_ring.blocks[r][:, :width] for r in offsets})
    hits_all = blockwise(hits_of).astype(f32)
    counts = jnp.sum(hits_all[:, experts_all : experts_all + 1] * hits_all, axis=0)
    count_total = sum_over(counts[:experts_all], "dp")
    n_valid = jnp.sum(lengths).astype(f32)
    fraction = count_total / (TOPK * n_valid)
    cot_rows = to_rows(cotangent)
    cot_ring = Gather(cot_rows, order, "ring_cotangent")
    cot_ring.step(normed_all)

    project = dot_nn(normed_all, w_qkv).reshape(n_expert, seq_count, slot_count, 3 * cols)
    attended = attend(owners, project, cosine, sine, key_live, head_gains)
    w_out = lax.all_gather(after(w_out, attended), "dp", axis=0, tiled=True)
    attended = after(attended, cot_ring.blocks[1], cot_ring.blocks[-1])
    cot_ring.step(attended)
    attended_low = lax.all_to_all(
        attended.reshape(n_expert, tok_rows, cols), "expert", split_axis=0, concat_axis=0, tiled=True
    )
    attended_low = jnp.swapaxes(attended_low, 0, 1).reshape(tok_rows, width)
    residual = inputs + dot_nn(attended_low, w_out)
    ffn_normed, ffn_back = jax.vjp(norm_rows, residual, ffn_gain)
    ffn_low = ffn_normed.astype(bf16)
    for _ in range(half - 3):
        cot_ring.step(residual)
    ffn_ring = Gather(ffn_low, order, "ring_ffn")
    ffn_ring.step()

    live = valid_rows[:, None]
    router_probs = jax.nn.softmax(dot_nn(ffn_low, router_weight), axis=-1)
    picked = chosen * router_probs
    picked_total = jnp.sum(picked, axis=-1, keepdims=True)
    prob_sums = jnp.sum(live * router_probs, axis=0)
    groups = [[0]] + [[-s, s] for s in range(1, half)] + [[half]]
    bases = [(n_expert - 2) * tok_rows]
    bases += [2 * s * tok_rows for s in range(half - 1)] + [(n_expert - 1) * tok_rows]
    w_down = expert_out.reshape(experts_here * FF, width)
    all_rows = n_expert * tok_rows

    def split(rows, group):
        return {r: rows[i * tok_rows : (i + 1) * tok_rows] for i, r in enumerate(group)}

    held, mix_blocks, group_gates = [], {}, []
    for i, g in enumerate(groups):
        *held, gates, mixed = experts_forward(
            [
                after(ffn_ring.blocks[r], cot_ring.blocks[half - 1], cot_ring.blocks[1 - half])
                if i == 2
                else ffn_ring.blocks[r]
                for r in g
            ],
            jnp.concatenate([hits_of[r] for r in g], axis=0),
            router_pad,
            own_rows,
            experts_all,
            expert_in,
            w_down,
            held,
            bases[i],
            all_rows,
        )
        group_gates.append(gates)
        mix_blocks.update(split(mixed, g))
        if i < half - 1:
            ffn_ring.step(mixed)
        if i == half - 1:
            ffn_ring.join()
        if i == 1:
            cot_ring.step(mixed)
    cot_ring.join(gates)
    x_all, gate_all, up_all, gated_all = held
    held, ffn_sum = [], None
    mix_sum = Scatter(mix_blocks[half], order, "ring_mixture")
    ready = ()
    for i in reversed(range(len(groups))):
        g = groups[i]
        *held, scores, grads = experts_backward(
            [cot_ring.blocks[r] for r in g],
            after(group_gates[i], *ready) if ready else group_gates[i],
            own_rows,
            gate_all,
            up_all,
            expert_in,
            w_down,
            held,
            bases[i],
        )
        grads = jnp.concatenate([grads, scores.astype(bf16)], axis=1)
        if i == half:
            ffn_sum = Scatter(grads, order, "ring_ffn_grad")
        elif i > 0:
            ffn_sum.step(grads[tok_rows:], grads[:tok_rows])
        if 2 < i < half:
            mix_sum.step(mix_blocks[i], mix_blocks[-i], grads)
        ready = (*mix_sum.sent, *ffn_sum.sent)
    out_all, gate_grad_all, up_grad_all = held
    sums = [
        GroupSum(gated_all, out_all, experts_here, "weights_out"),
        GroupSum(x_all, gate_grad_all, 1, "weights_gate"),
        GroupSum(x_all, up_grad_all, 1, "weights_up"),
    ]
    mix_sum.step(mix_blocks[2], mix_blocks[-2], grads)
    sums[0].first(*mix_sum.sent)
    ffn_grad = ffn_sum.finish(after(grads, sums[0].far))
    gate_grads = ffn_grad[:, width : width + experts_all] * chosen
    ffn_grad = ffn_grad[:, :width]
    picked_grad = (
        live
        * chosen
        * (
            gate_grads / picked_total
            - jnp.sum(gate_grads * picked, axis=-1, keepdims=True) / (picked_total * picked_total)
        )
    )
    prob_grad = picked_grad + balance_coef * experts_all * fraction[None, :] / n_valid * live
    logit_grad = router_probs * (
        prob_grad - jnp.sum(router_probs * prob_grad, axis=-1, keepdims=True)
    )
    ffn_grad = ffn_grad + jnp.dot(logit_grad, router_weight.astype(f32).T, precision=PRECISE)
    router_terms = jnp.dot(ffn_low.astype(f32).T, logit_grad, precision=PRECISE)
    residual_norm_grad, ffn_gain_terms = ffn_back(ffn_grad)
    residual_grad = cot_rows.astype(f32) * live + residual_norm_grad
    branch_grad = residual_grad.astype(bf16)

    attended_grad = dot_nt(branch_grad, w_out).astype(bf16)
    attended_grad = lax.all_to_all(
        jnp.swapaxes(attended_grad.reshape(tok_rows, n_expert, cols), 0, 1),
        "expert",
        split_axis=0,
        concat_axis=0,
        tiled=True,
    ).reshape(attended.shape)

    output_terms = dot_tn(attended_low, branch_grad).astype(bf16)
    out_share = lax.psum_scatter(output_terms, "dp", scatter_dimension=0, tiled=True)
    sums[0].second(branch_grad)
    attended_grad = after(attended_grad, sums[0].near, output_terms)

    mix_sum.step(mix_blocks[1], mix_blocks[-1], attended_grad)
    attended_grad = after(attended_grad, *mix_sum.sent)
    proj_grad, gain_parts = attend_back(
        owners, project, attended_grad, cosine, sine, key_live, head_gains
    )
    proj_grad = proj_grad.reshape(all_rows, 3 * cols)
    normed_terms = dot_nt(proj_grad, w_qkv).astype(bf16)
    block_rows = residual + mix_sum.finish(mix_blocks[0])
    normed_terms = after(normed_terms, block_rows)
    normed_parts = {
        r: normed_terms[i * tok_rows : (i + 1) * tok_rows] for i, r in enumerate(offsets)
    }
    normed_sum = Scatter(normed_parts[half], order, "ring_normed_grad")
    attn_gain_terms = (
        jnp.sum(normed_terms.astype(f32) * normed_all.astype(f32), axis=0) / attn_gain
    )
    head_gain_grads = jnp.sum(gain_parts, axis=(0, 1)).reshape(-1)
    small = Sum(
        jnp.concatenate(
            [
                router_terms.reshape(-1),
                ffn_gain_terms,
                attn_gain_terms,
                head_gain_grads,
                prob_sums,
            ]
        )
    )
    sums[1].first(normed_terms)
    waits = [sums[1].far]
    for s in range(half - 1, 0, -1):
        normed_sum.step(normed_parts[s], normed_parts[-s], *waits)
        waits = []
        if s == half - 1:
            sums[1].second(normed_terms)
            proj_terms = dot_tn(after(normed_all, sums[1].near), proj_grad).astype(bf16)
            waits = [sums[1].near, proj_terms]
        if s == half - 2:
            sums[2].first(proj_terms)
            waits = [sums[2].far]
        if s == half - 3:
            sums[2].second(proj_terms)
    proj_share = lax.psum_scatter(proj_terms, "dp", scatter_dimension=0, tiled=True)
    normed_grad = normed_sum.finish(after(normed_parts[0], sums[2].near))
    grad_out = lax.psum_scatter(
        out_share, "expert", scatter_dimension=0, tiled=True
    ).astype(f32)
    (input_norm_grad,) = jax.vjp(lambda v: norm_rows(v, attn_gain), inputs)[1](normed_grad)
    grad_tokens = from_rows(residual_grad + input_norm_grad)
    block_out = from_rows(block_rows)
    grad_expert_out = sums[0].total().reshape(experts_here, -1, width)
    shares = [sums[1].total(), sums[2].total()]
    grad_expert_in = jnp.stack(
        [
            jnp.concatenate([s[:, e * FF : (e + 1) * FF] for s in shares], axis=1)
            for e in range(experts_here)
        ]
    )

    grad_qkv = lax.all_to_all(
        proj_share.reshape(n_expert, row_count, 3 * cols),
        "expert",
        split_axis=0,
        concat_axis=0,
        tiled=True,
    ).reshape(n_expert, row_count, heads_here, 3, HD)
    grad_qkv = grad_qkv.transpose(1, 3, 0, 2, 4).reshape(row_count, 3, width).astype(f32)

    small.step(normed_grad)
    small.step(grad_qkv)
    small = small.finish()
    places, pieces = 0, []
    for size in (width * experts_all, width, width, HD, HD, experts_all):
        pieces.append(small[places : places + size])
        places += size
    grad_router, grad_ffn_gain, grad_attn_gain, grad_q_gain, grad_k_gain, prob_total = pieces
    balance_loss = balance_coef * experts_all * jnp.sum(fraction * (prob_total / n_valid))
    return (
        block_out,
        balance_loss,
        grad_tokens,
        grad_attn_gain,
        grad_q_gain,
        grad_k_gain,
        grad_qkv,
        grad_out,
        grad_ffn_gain,
        grad_router.reshape(width, experts_all),
        grad_expert_in,
        grad_expert_out,
    )


def solution(mesh):
    placed = (
        P("dp", "expert", None, None),
        P(),
        P("dp", "expert", None, None),
        P(),
        P(),
        P(),
        P(("dp", "expert"), None, None),
        P(("dp", "expert"), None),
        P(),
        P(),
        P("expert", None, None),
        P("expert", None, None),
        P(),
        P("dp", "expert", None, None),
    )
    return jax.shard_map(
        body,
        mesh=mesh,
        in_specs=placed,
        out_specs=(
            P("dp", "expert", None, None),
            P(),
            P("dp", "expert", None, None),
            P(),
            P(),
            P(),
            P(("dp", "expert"), None, None),
            P(("dp", "expert"), None),
            P(),
            P(),
            P("expert", "dp", None),
            P("expert", "dp", None),
        ),
        check_vma=False,
    )
```
